128 devices in a mesh: grp: 16 (over z, x), in: 8 (over y, core).
Axes of the slice: x: 4, y: 4, z: 4, core: 2. Of those that a mesh axis runs over, the one named last changes fastest.
Arguments:
- encoded: bfloat16 [16384, 1024], P(('grp', 'in')), may hold values from -6 to 6
- owner_slot: int32 [16384], P(('grp', 'in')), may hold values from 0 to 16383, as said below
- label_mask: int32 [16384], P(('grp', 'in')), may hold values 0 or 1
- cotangent: bfloat16 [16384, 1024], P(('grp', 'in')), may hold values from -6 to 6
- weight: bfloat16 [1024, 1024], P(('grp', 'in')), may hold values from -0.1875 to 0.1875
- block_cols: int32 [128, 10], P(('grp', 'in')), may hold values from 0 to 7, as said below
- block_counts: int32 [128], P(('grp', 'in')), may hold values from 1 to 10, as said below
- block_values: bfloat16 [128, 10, 128, 128], P(('grp', 'in')), as said below
Outputs:
- layer_out: bfloat16 [16384, 1024], P(('grp', 'in'))
- encoded_grad: bfloat16 [16384, 1024], P(('grp', 'in'))
- weight_grad: float32 [1024, 1024], P(('grp', 'in'))
The draws below stay inside these ranges and needn't reach their ends.
Inputs may be any that keep to these rules, and one draw needn't show every extreme that they name: A permutation of the nodes. The owner of node i is owner_slot[i] // 128; from the nodes of one device at most 2 go to one owner, and every device sends exactly 2 to some owner. `block_cols`: slot 0 of every block-row names the block-row itself; slots at or past block_counts are unused. adjacency is symmetric. `block_counts`: every partition group has a block-row with 10 slots in use. `block_values`: the blocks make adjacency symmetric.
All inputs are finite; a program needn't handle non-finite values. No bound on the sum of `label_mask` on one device may be relied on, other than what follows from the above.
Results may differ from the reference program's by a relative error of at most 0.0063.
Values may be sent and summed in bfloat16 or wider, within the bound.
A program may use at most 64 MiB of HBM per device.

```python
import jax
import jax.numpy as jnp
from jax import lax

D = 1024
ROWS_DEV = 128
BLK = 128
NB = 10
OWNERS = 128
NODES = 16384
GROUP_BLOCKS = 8
BLOCK_ROWS = 128
N_GRP = 16
N_IN = 8


def draw_owner_slot(key, part):
    key = jax.random.fold_in(key, 7)
    order_key, shift_key, source_key, owner_key = jax.random.split(key, 4)
    owners = N_GRP * N_IN
    fair_share = ROWS_DEV // owners
    half_count = owners // 2
    slot_order = jax.random.permutation(order_key, owners).astype(jnp.int32)
    shift_size = jax.random.randint(shift_key, (half_count,), 0, fair_share + 1).astype(jnp.int32)
    shift_size = shift_size.at[0].set(fair_share)
    amount = jnp.zeros((owners,), jnp.int32).at[slot_order].set(fair_share + jnp.concatenate([shift_size, -shift_size]))
    bounds = jnp.cumsum(amount).astype(jnp.int32)
    position = jnp.arange(ROWS_DEV, dtype=jnp.int32)
    offset = jnp.sum((position[:, None] >= bounds[None, :]).astype(jnp.int32), axis=1)
    source = jnp.arange(owners, dtype=jnp.int32)
    target_rows = (source[:, None] + offset[None, :]) % owners

    def shuffle(sub_key):
        return jax.random.permutation(sub_key, ROWS_DEV).astype(jnp.int32)
    source_perm = jax.vmap(shuffle)(jax.random.split(source_key, owners))
    owner_perm = jax.vmap(shuffle)(jax.random.split(owner_key, owners))
    landing = owner_perm[target_rows, position[None, :]]
    slot_value = target_rows * ROWS_DEV + landing
    slot_index = source[:, None] * ROWS_DEV + source_perm
    return jnp.zeros((owners * ROWS_DEV,), jnp.int32).at[slot_index.reshape(-1)].set(slot_value.reshape(-1))


def block_plan(key):
    layout_random_seed = jax.random.fold_in(key, 101)
    shuffle_random_seed, presence_random_seed, central_vertex_seed = jax.random.split(layout_random_seed, 3)
    exchange_round_total = NB - 1
    each_cluster_share = N_IN * ROWS_DEV // BLK

    def shuffle(sub_key):
        return jax.random.permutation(sub_key, each_cluster_share).astype(jnp.int32)
    pairing = jax.vmap(shuffle)(jax.random.split(shuffle_random_seed, N_GRP * exchange_round_total)).reshape(N_GRP, exchange_round_total, each_cluster_share)
    inverse = jnp.argsort(pairing, axis=-1).astype(jnp.int32)
    partner = jnp.take_along_axis(pairing, inverse ^ 1, axis=-1)
    leading = inverse % 2 == 0
    edge_id = inverse // 2
    active_arc_mask = jax.random.randint(presence_random_seed, (N_GRP, exchange_round_total, each_cluster_share // 2), 0, 4) > 0
    hub_row = jax.random.randint(central_vertex_seed, (N_GRP, 1, 1), 0, each_cluster_share).astype(jnp.int32)
    hub_edge = jnp.take_along_axis(edge_id, jnp.broadcast_to(hub_row, (N_GRP, exchange_round_total, 1)), axis=-1)
    active_arc_mask = active_arc_mask | (jnp.arange(each_cluster_share // 2, dtype=jnp.int32)[None, None, :] == hub_edge)
    row_live = jnp.take_along_axis(active_arc_mask, edge_id, axis=-1)
    self_col = jnp.broadcast_to(jnp.arange(each_cluster_share, dtype=jnp.int32)[None, :, None], (N_GRP, each_cluster_share, 1))
    cols_all = jnp.concatenate([self_col, jnp.transpose(partner, (0, 2, 1))], axis=-1)
    live_all = jnp.concatenate([jnp.ones((N_GRP, each_cluster_share, 1), bool), jnp.transpose(row_live, (0, 2, 1))], axis=-1)
    sort_key = jnp.where(live_all, 0, NB) + jnp.arange(NB, dtype=jnp.int32)[None, None, :]
    slot_order = jnp.argsort(sort_key, axis=-1).astype(jnp.int32)
    plan_cols = jnp.take_along_axis(cols_all, slot_order, axis=-1)
    counts = jnp.sum(live_all.astype(jnp.int32), axis=-1)
    return (plan_cols, counts, slot_order, edge_id, leading)


def draw_block_cols(key, part):
    plan_cols, counts, slot_order, edge_id, leading = block_plan(key)
    return plan_cols.reshape(BLOCK_ROWS, NB).astype(jnp.int32)


def draw_block_counts(key, part):
    plan_cols, counts, slot_order, edge_id, leading = block_plan(key)
    return counts.reshape(BLOCK_ROWS).astype(jnp.int32)


def draw_block_values(key, part):
    plan_cols, counts, slot_order, edge_id, leading = block_plan(key)
    value_key = jax.random.fold_in(key, 29)
    edge_key, self_key = jax.random.split(value_key, 2)
    exchange_round_total = NB - 1
    each_cluster_share = N_IN * ROWS_DEV // BLK
    value_scale = (0.8 * NB * BLK) ** (-0.5)
    shape_edge = (N_GRP, exchange_round_total, each_cluster_share // 2, BLK, BLK)
    shape_self = (N_GRP, each_cluster_share, BLK, BLK)
    edge_vals = jax.random.normal(edge_key, shape_edge) * value_scale
    self_raw = jax.random.normal(self_key, shape_self)
    self_vals = (self_raw + jnp.swapaxes(self_raw, -1, -2)) * (0.7071 * value_scale)
    group_ix = jnp.arange(N_GRP)[:, None, None]
    hop_ix = jnp.arange(exchange_round_total)[None, :, None]
    picked = edge_vals[group_ix, hop_ix, edge_id]
    oriented = jnp.where(leading[..., None, None], picked, jnp.swapaxes(picked, -1, -2))
    stacked = jnp.concatenate([self_vals[:, :, None], jnp.transpose(oriented, (0, 2, 1, 3, 4))], axis=2)
    row_ix = jnp.arange(each_cluster_share)[None, :, None]
    ordered = stacked[group_ix, row_ix, slot_order]
    return ordered.reshape(BLOCK_ROWS, NB, BLK, BLK).astype(jnp.bfloat16)


def plant(array, own_key, low, top_value):
    longest = array.shape.index(max(array.shape))
    spots = []
    for shift in (0, 1):
        where = [jax.random.randint(jax.random.fold_in(own_key, axis), (), 0, length) for axis, length in enumerate(array.shape)]
        where[longest] = (where[longest] + shift) % array.shape[longest]
        spots.append(tuple(where))
    return array.at[spots[0]].set(low).at[spots[1]].set(top_value)


def block_scale(key, shape, cuts, low, top_value):
    def one(dim, shards_of):
        draws = jax.random.uniform(jax.random.fold_in(jax.random.fold_in(key, 6), dim), (shards_of,), jnp.float32, low / len(cuts), top_value / len(cuts))
        return jnp.repeat(jnp.exp(draws), shape[dim] // shards_of).reshape((-1,) + (1,) * (len(shape) - dim - 1))

    factor_of = one(*cuts[0])
    for cut in cuts[1:]:
        factor_of = factor_of * one(*cut)
    return factor_of


def normal_values(stream_key, shape, spread, bound, cuts=(), kind=jnp.bfloat16):
    loudness = block_scale(stream_key, shape, cuts, -0.22, 0.18) if cuts else 1.0
    array = jax.random.normal(stream_key, shape, jnp.float32) * spread * loudness
    return jnp.minimum(jnp.maximum(array, -bound), bound).astype(kind)


def setup_inputs(seed: int = 0) -> dict:
    seeds = jax.random.split(jax.random.key(seed), 9)
    encoded = normal_values(seeds[0], (NODES, D), 1.0, 6.0, ((0, 128),))
    owner_slot = draw_owner_slot(jax.random.fold_in(seeds[8], 71), 0)
    label_mask = plant((jax.random.randint(seeds[2], (NODES,), 0, 2) < 1).astype(jnp.int32), jax.random.fold_in(seeds[2], 1), 0, 1)
    cotangent = normal_values(seeds[3], (NODES, D), 1.0, 6.0, ((0, 128),))
    weight = normal_values(seeds[4], (D, D), D ** -0.5, 0.1875, ((0, 128),))
    block_cols = draw_block_cols(jax.random.fold_in(seeds[8], 71), 0)
    block_counts = draw_block_counts(jax.random.fold_in(seeds[8], 71), 0)
    block_values = draw_block_values(jax.random.fold_in(seeds[8], 71), 0)
    return dict(encoded=encoded, owner_slot=owner_slot, label_mask=label_mask, cotangent=cotangent, weight=weight, block_cols=block_cols, block_counts=block_counts, block_values=block_values)


def smooth_gate(values):
    return jax.nn.gelu(values, approximate=True)

def forward_group(input_rows):
    group_feed, group_cols, group_value_rows = input_rows
    block_list = group_feed.reshape(GROUP_BLOCKS, BLK, D)
    picked = block_list[group_cols]
    mixed_block = jnp.einsum('bkpq,bkqd->bpd', group_value_rows.astype(jnp.float32), picked.astype(jnp.float32), precision=lax.Precision.HIGHEST)
    return mixed_block.reshape(GROUP_BLOCKS * BLK, D)

def group_backward_pass(input_rows):
    group_feed, group_cols, group_value_rows = input_rows
    block_list = group_feed.reshape(GROUP_BLOCKS, BLK, D)
    contribution_terms = jnp.einsum('uano,uni->uaoi', group_value_rows.astype(jnp.float32), block_list.astype(jnp.float32), precision=lax.Precision.HIGHEST)
    summed = jax.ops.segment_sum(contribution_terms.reshape(GROUP_BLOCKS * NB, BLK, D), group_cols.reshape(-1).astype(jnp.int32), num_segments=GROUP_BLOCKS)
    return summed.reshape(GROUP_BLOCKS * BLK, D)

def reference(encoded, owner_slot, label_mask, cotangent, weight, block_cols, block_counts, block_values):
    own_rows = jnp.zeros_like(encoded).at[owner_slot].set(encoded)
    labelled = jnp.where(label_mask[:, None] > 0, cotangent, jnp.zeros_like(cotangent))
    own_cot = jnp.zeros_like(cotangent).at[owner_slot].set(labelled)
    live_slot = jnp.arange(NB, dtype=jnp.int32)[None, :] < block_counts[:, None]
    masked = jnp.where(live_slot[:, :, None, None], block_values, jnp.zeros_like(block_values))
    cols_grouped = block_cols.reshape(N_GRP, GROUP_BLOCKS, NB)
    vals_grouped = masked.reshape(N_GRP, GROUP_BLOCKS, NB, BLK, BLK)
    mixed_rows = lax.map(forward_group, (own_rows.reshape(N_GRP, GROUP_BLOCKS * BLK, D), cols_grouped, vals_grouped))
    mixed_rows = mixed_rows.reshape(NODES, D).astype(jnp.bfloat16)
    pre_act = jnp.dot(mixed_rows, weight, preferred_element_type=jnp.float32)
    activated, pullback = jax.vjp(smooth_gate, pre_act)
    out_own = activated.astype(jnp.bfloat16)
    layer_out = out_own[owner_slot]
    grad_pre = pullback(own_cot.astype(jnp.float32))[0].astype(jnp.bfloat16)
    weight_grad = lax.dot_general(mixed_rows, grad_pre, (((0,), (0,)), ((), ())), preferred_element_type=jnp.float32) / OWNERS
    grad_feed = lax.dot_general(grad_pre, weight, (((1,), (1,)), ((), ())), preferred_element_type=jnp.float32).astype(jnp.bfloat16)
    grad_own = lax.map(group_backward_pass, (grad_feed.reshape(N_GRP, GROUP_BLOCKS * BLK, D), cols_grouped, vals_grouped))
    grad_own = grad_own.reshape(NODES, D).astype(jnp.bfloat16)
    encoded_grad = grad_own[owner_slot]
    return (layer_out, encoded_grad, weight_grad)
```

```python
import functools

import jax
import jax.numpy as jnp
from jax import lax
from jax.experimental import pallas as pl
from jax.experimental.pallas import tpu as pltpu
from jax.sharding import PartitionSpec as P

MESH = pl.DeviceIdType.MESH
BF = jnp.bfloat16
F32 = jnp.float32
I32 = jnp.int32

NG = 16
NI = 8
ROWS = 128
D = 1024
SLOTS = 256


def iota(shape, dim):
    return lax.broadcasted_iota(I32, shape, dim)


def ones_where(cond):
    return jnp.where(cond, 1.0, 0.0).astype(BF)


def dot(a, b):
    return jnp.dot(a, b, preferred_element_type=F32)


def dot_t0(a, b):
    return lax.dot_general(a, b, (((0,), (0,)), ((), ())), preferred_element_type=F32)


def dot_t1(a, b):
    return lax.dot_general(a, b, (((1,), (1,)), ((), ())), preferred_element_type=F32)


def kernel(
    cols_ref, count_ref, enc_ref, slot_ref, mask_ref, cot_ref, w_ref, val_ref,
    out_ref, grad_ref, wgrad_ref,
    s_rows, r_rows, s_pl, r_pl, s_cot, r_cot,
    w_f32, w_got, whole_w, adj,
    q_rows, x_slots, v_all, q_cot, c_slots, place,
    mixed, mixed_sib, mixed_rows,
    g_half, g_all, gf_out, gf_in,
    o_slots, o_mid, o_send, o_back,
    z_slots, z_mid, z_send, z_back,
    wg, wg_in, wg_sum, wg_out,
    rows_s, rows_r, pl_s, pl_r, cot_s, cot_r,
    w0_s, w0_r, w1_s, w1_r, w2_s, w2_r, w3_s, w3_r,
    a_s, a_r, f_s, f_r,
    x_s, x_r, v_s, v_r, c_s, c_r,
    m_s, m_r, ms_s, ms_r,
    g_s, g_r, gf_s, gf_r,
    o1_s, o1_r, o2_s, o2_r,
    z1_s, z1_r, z2_s, z2_r,
    rs_s, rs_r, t_s, t_r,
):
    mg = lax.axis_index("grp")
    mi = lax.axis_index("in")
    core = lax.rem(mi, 2)
    my_y = lax.div(mi, 2)
    sib = mi + 1 - 2 * core

    def grp_to(p):
        return lax.rem(mg + p, NG)

    def grp_from(p):
        return lax.rem(mg + NG - p, NG)

    def in_to(p):
        return lax.rem(mi + p, NI)

    def in_from(p):
        return lax.rem(mi + NI - p, NI)

    def rcopy(src, dst, ss, rs, dev):
        return pltpu.make_async_remote_copy(
            src_ref=src, dst_ref=dst, send_sem=ss, recv_sem=rs, device_id=dev, device_id_type=MESH
        )

    def got(dst, ss, rs):
        rcopy(dst, dst, ss, rs, (mg, sib)).wait_recv()

    def sent(src, ss, rs):
        rcopy(src, src, ss, rs, (mg, sib)).wait_send()

    def each(n, body):
        def step(p, carry):
            body(p)
            return carry

        lax.fori_loop(1, n, step, 0)

    t_grp = 4 * my_y + lax.div(mg, 4)
    t_in = 2 * lax.rem(mg, 4)
    from_grp = 4 * lax.rem(mg, 4) + my_y
    from_in = 2 * lax.div(mg, 4)
    half = core
    t_self = jnp.logical_and(t_grp == mg, lax.div(t_in, 2) == my_y)

    barrier = pltpu.get_barrier_semaphore()

    def greet(dev):
        pl.semaphore_signal(barrier, inc=1, device_id=dev, device_id_type=MESH)

    each(NG, lambda p: greet((grp_to(p), mi)))
    each(NI, lambda p: greet((mg, in_to(p))))
    for c in range(2):
        @pl.when(jnp.logical_not(jnp.logical_and(t_self, core == c)))
        def _():
            greet((from_grp, from_in + c))

    slot_row = slot_ref[...]
    eye = iota((ROWS, ROWS), 0) == iota((ROWS, ROWS), 1)
    slot_b = jnp.broadcast_to(slot_row, (ROWS, ROWS))
    slot_col = jnp.sum(jnp.where(eye, slot_b, 0), axis=1, keepdims=True)
    own_b = lax.shift_right_logical(slot_b, 7)
    own_col = lax.shift_right_logical(slot_col, 7)
    same = own_b == jnp.broadcast_to(own_col, (ROWS, ROWS))
    n_ix, m_ix = iota((ROWS, ROWS), 0), iota((ROWS, ROWS), 1)
    rank_row = jnp.sum(jnp.where(same & (n_ix < m_ix), 1, 0), axis=0, keepdims=True)
    rank_col = jnp.sum(jnp.where(same & (m_ix < n_ix), 1, 0), axis=1, keepdims=True)
    flat_row = lax.shift_right_logical(slot_row, 7) * 2 + rank_row
    flat_col = own_col * 2 + rank_col
    spread = iota((SLOTS, ROWS), 0) == jnp.broadcast_to(flat_row, (SLOTS, ROWS))
    collect = ones_where(
        iota((ROWS, SLOTS), 1) == jnp.broadcast_to(flat_col, (ROWS, SLOTS))
    )
    spread_rows = ones_where(spread)
    s_rows[...] = dot(spread_rows, enc_ref[...]).astype(BF).reshape(NG, 16, D)
    place1 = jnp.bitwise_and(slot_col, ROWS - 1) + 1
    place_b = jnp.broadcast_to(place1, (ROWS, ROWS)).astype(F32).astype(BF)
    s_pl[...] = dot(spread_rows, place_b).astype(BF).reshape(NG, 16, ROWS)

    n_send = jnp.where(t_self, 1, 2)
    pl.semaphore_wait(barrier, (NG - 1) + (NI - 1) + n_send)

    def grp_copy(src, dst, ss, rs):
        def go(p):
            rcopy(src.at[grp_to(p)], dst.at[mg], ss.at[p], rs.at[p], (grp_to(p), mi)).start()

        each(NG, go)

    def grp_got(dst, ss, rs):
        each(NG, lambda p: got(dst.at[grp_from(p)], ss.at[p], rs.at[p]))

    def grp_sent(src, ss, rs):
        each(NG, lambda p: sent(src.at[grp_to(p)], ss.at[p], rs.at[p]))

    def in_copy(src, dst, ss, rs):
        def go(p):
            rcopy(src(in_to(p)), dst(mi), ss.at[p], rs.at[p], (mg, in_to(p))).start()

        each(NI, go)

    def in_got(dst, ss, rs):
        each(NI, lambda p: got(dst(in_from(p)), ss.at[p], rs.at[p]))

    def in_sent(src, ss, rs):
        each(NI, lambda p: sent(src(in_to(p)), ss.at[p], rs.at[p]))

    grp_copy(s_pl, r_pl, pl_s, pl_r)
    grp_copy(s_rows, r_rows, rows_s, rows_r)
    r_pl[mg] = s_pl[mg]
    r_rows[mg] = s_rows[mg]

    w_f32[...] = w_ref[...].astype(F32)
    w0 = rcopy(w_f32, w_got, w0_s, w0_r, (mg, sib))
    w0.start()

    count = count_ref[0]
    for c in range(NI):
        acc = jnp.zeros((ROWS, ROWS), F32)
        for k in range(10):
            live = jnp.logical_and(cols_ref[0, k] == c, count > k)
            acc = acc + jnp.where(live, val_ref[k].astype(F32), 0.0)
        adj[mi, :, c * 128:(c + 1) * 128] = acc.astype(BF)
    rcopy(adj.at[mi], adj.at[mi], a_s.at[0], a_r.at[0], (mg, sib)).start()

    def y_to(q):
        return lax.rem(mi + 2 * q, NI)

    def y_from(q):
        return lax.rem(mi + NI - 2 * q, NI)

    def send_adj(q):
        rcopy(adj.at[mi], adj.at[mi], a_s.at[q], a_r.at[q], (mg, y_to(q))).start()

    each(4, send_adj)

    spread_cot = ones_where(spread & (jnp.broadcast_to(mask_ref[...], (SLOTS, ROWS)) > 0))
    s_cot[...] = dot(spread_cot, cot_ref[...]).astype(BF).reshape(NG, 16, D)
    grp_copy(s_cot, r_cot, cot_s, cot_r)
    r_cot[mg] = s_cot[mg]

    w0.wait()
    first = core == 0
    pair = jnp.concatenate(
        [
            jnp.where(first, w_f32[...], w_got[...]),
            jnp.where(first, w_got[...], w_f32[...]),
        ],
        axis=0,
    )
    pair = jnp.where(first, pair[:, :512], pair[:, 512:]).astype(BF)
    whole_w[core, mg * 4 + my_y] = pair

    def w1_copy(q):
        ref = whole_w.at[core, mg * 4 + my_y]
        rcopy(ref, ref, w1_s.at[q], w1_r.at[q], (mg, y_to(q))).start()

    each(4, w1_copy)

    r_ix, c_ix = iota((SLOTS, SLOTS), 0), iota((SLOTS, SLOTS), 1)

    def moved(ix):
        return (
            lax.shift_right_logical(jnp.bitwise_and(ix, 31), 1) * 16
            + lax.shift_right_logical(ix, 5) * 2
            + jnp.bitwise_and(ix, 1)
        )

    perm = ones_where(c_ix == moved(r_ix))
    perm_t = ones_where(r_ix == moved(c_ix))
    low = (jnp.bitwise_and(r_ix, 31) == jnp.bitwise_and(c_ix, 31)) & (
        lax.shift_right_logical(c_ix, 5) == mi
    )
    o_rows = ones_where(
        iota((16, SLOTS), 0) == lax.shift_right_logical(iota((16, SLOTS), 1), 5)
    )

    grp_got(r_pl, pl_s, pl_r)
    pl_cols = dot(perm, r_pl[...].reshape(SLOTS, ROWS))
    pl_wide = jnp.concatenate([pl_cols, pl_cols], axis=1)
    v_all[mi] = dot(o_rows, jnp.where(low, pl_wide, 0.0).astype(BF)).astype(BF)
    in_copy(lambda i: v_all.at[mi], lambda i: v_all.at[i], v_s, v_r)
    grp_got(r_rows, rows_s, rows_r)
    for f in range(NI):
        part = r_rows[:, :, f * 128:(f + 1) * 128].reshape(SLOTS, 128)
        q_rows[f] = dot(perm, part).astype(BF).reshape(NI, 32, 128)
    in_copy(lambda i: q_rows.at[i], lambda i: x_slots.at[:, i], x_s, x_r)
    x_slots[:, mi] = q_rows[mi]

    each(4, lambda q: got(whole_w.at[core, mg * 4 + y_from(q) // 2], w1_s.at[q], w1_r.at[q]))

    def w2_copy(p):
        ref = whole_w.at[core, pl.ds(mg * 4, 4)]
        rcopy(ref, ref, w2_s.at[p], w2_r.at[p], (grp_to(p), mi)).start()

    each(NG, w2_copy)

    def hand_on(q):
        ref = adj.at[y_from(q)]
        got(ref, a_s.at[q], a_r.at[q])
        rcopy(ref, ref, f_s.at[q], f_r.at[q], (mg, sib)).start()

    each(4, hand_on)

    grp_got(r_cot, cot_s, cot_r)
    q_cot[...] = dot(perm, r_cot[...].reshape(SLOTS, D)).astype(BF).reshape(NI, 32, D)
    in_copy(lambda i: q_cot.at[i], lambda i: c_slots.at[i], c_s, c_r)
    c_slots[mi] = q_cot[mi]

    in_got(lambda i: v_all.at[i], v_s, v_r)
    v_sum = v_all[0].astype(F32)
    for i in range(1, NI):
        v_sum = v_sum + v_all[i].astype(F32)
    node1 = (iota((ROWS, SLOTS), 0) + 1).astype(F32)
    for o in range(NI):
        place[o] = ones_where(node1 == jnp.broadcast_to(v_sum[o:o + 1, :], (ROWS, SLOTS)))

    got(adj.at[sib], a_s.at[0], a_r.at[0])
    each(4, lambda q: got(adj.at[lax.rem(sib + NI - 2 * q, NI)], f_s.at[q], f_r.at[q]))
    in_got(lambda i: x_slots.at[:, i], x_s, x_r)
    feats = jnp.concatenate(
        [dot(place[o], x_slots[o].reshape(SLOTS, 128)).astype(BF) for o in range(NI)], axis=0
    )
    for o in range(NI):
        mixed[o] = dot(adj[o], feats).astype(BF)
    in_copy(
        lambda i: mixed.at[i],
        lambda i: mixed_rows.at[:, pl.ds(pl.multiple_of(i * 128, 128), 128)],
        m_s, m_r,
    )
    ms = rcopy(mixed, mixed_sib, ms_s, ms_r, (mg, sib))
    ms.start()
    mixed_rows[:, pl.ds(pl.multiple_of(mi * 128, 128), 128)] = mixed[mi]

    each(NG, lambda p: got(whole_w.at[core, pl.ds(grp_from(p) * 4, 4)], w2_s.at[p], w2_r.at[p]))
    w3 = rcopy(whole_w.at[core], whole_w.at[core], w3_s, w3_r, (mg, sib))
    w3.start()

    in_got(lambda i: c_slots.at[i], c_s, c_r)
    own_cot = dot(place[mi], c_slots[...].reshape(SLOTS, D))

    got(whole_w.at[1 - core], w3_s, w3_r)
    in_got(
        lambda i: mixed_rows.at[:, pl.ds(pl.multiple_of(i * 128, 128), 128)], m_s, m_r
    )
    rows_val = mixed_rows[...]
    for h in range(2):
        v = dot(rows_val, whole_w[h].reshape(D, 512))
        k0 = 0.7978845608028654
        th = jnp.tanh(k0 * (v + 0.044715 * (v * v * v)))
        act = 0.5 * v * (1.0 + th)
        slope = 0.5 * (1.0 + th) + 0.5 * v * (1.0 - th * th) * (k0 * (1.0 + 3 * 0.044715 * (v * v)))
        o_mid_part = act.astype(BF)
        g_half[h] = (own_cot[:, h * 512:(h + 1) * 512] * slope).astype(BF)
        out_ref[:, h * 512:(h + 1) * 512] = o_mid_part

    for f in range(NI):
        w_rows = whole_w[:, f * 8:(f + 1) * 8]
        gf_out[f] = (
            dot_t1(g_half[0], w_rows[0].reshape(128, 512))
            + dot_t1(g_half[1], w_rows[1].reshape(128, 512))
        ).astype(BF)
    in_copy(lambda i: gf_out.at[i], lambda i: gf_in.at[i], gf_s, gf_r)
    gf_in[mi] = gf_out[mi]

    o_slots[...] = dot_t0(place[mi], out_ref[...]).astype(BF).reshape(NI, 32, D)
    in_copy(lambda i: o_slots.at[i], lambda i: o_mid.at[i], o1_s, o1_r)
    o_mid[mi] = o_slots[mi]

    in_copy(lambda i: g_half.at[lax.rem(i, 2)], lambda i: g_all.at[i], g_s, g_r)
    g_all[mi] = g_half[core]

    in_got(lambda i: gf_in.at[i], gf_s, gf_r)
    feed = gf_in[...].reshape(D, 128)
    for o in range(NI):
        back = dot(adj[o], feed).astype(BF)
        z_slots[:, o] = dot_t0(place[o], back).astype(BF).reshape(NI, 32, 128)
    in_copy(lambda i: z_slots.at[i], lambda i: z_mid.at[i], z1_s, z1_r)
    z_mid[mi] = z_slots[mi]

    in_got(lambda i: o_mid.at[i], o1_s, o1_r)
    o_send[...] = dot(perm_t, o_mid[...].reshape(SLOTS, D)).astype(BF).reshape(NG, 16, D)
    grp_copy(o_send, o_back, o2_s, o2_r)
    o_back[mg] = o_send[mg]

    in_got(lambda i: z_mid.at[i], z1_s, z1_r)
    for f in range(NI):
        z_send[:, :, f * 128:(f + 1) * 128] = (
            dot(perm_t, z_mid[f].reshape(SLOTS, 128)).astype(BF).reshape(NG, 16, 128)
        )
    grp_copy(z_send, z_back, z2_s, z2_r)
    z_back[mg] = z_send[mg]

    got(mixed_sib, ms_s, ms_r)
    in_got(lambda i: g_all.at[i], g_s, g_r)
    g_val = g_all[...].reshape(D, 512)
    mine = dot_t0(mixed[...].reshape(D, 128), g_val).reshape(8, 16, 512)
    other = dot_t0(mixed_sib[...].reshape(D, 128), g_val).reshape(8, 16, 512)
    wg[pl.ds(core * 8, 8)] = mine
    wg[pl.ds((1 - core) * 8, 8)] = other
    grp_copy(wg, wg_in, rs_s, rs_r)
    wg_in[mg] = wg[mg]
    grp_got(wg_in, rs_s, rs_r)
    total = wg_in[0]
    for g in range(1, NG):
        total = total + wg_in[g]
    total = total * (1.0 / 128)
    wg_sum[0] = total[:8]
    wg_sum[1] = total[8:]
    for h in range(2):
        @pl.when(jnp.logical_not(jnp.logical_and(t_self, core == h)))
        def _():
            rcopy(
                wg_sum.at[h], wg_out.at[core], t_s.at[h], t_r.at[core], (t_grp, t_in + h)
            ).start()

    @pl.when(t_self)
    def _():
        wg_out[core] = wg_sum[core]

    grp_got(o_back, o2_s, o2_r)
    out_ref[...] = dot(collect, o_back[...].reshape(SLOTS, D)).astype(BF)
    grp_got(z_back, z2_s, z2_r)
    grad_ref[...] = dot(collect, z_back[...].reshape(SLOTS, D)).astype(BF)

    for c in range(2):
        @pl.when(jnp.logical_not(jnp.logical_and(t_self, core == c)))
        def _():
            got(wg_out.at[c], t_s.at[c], t_r.at[c])
    wgrad_ref[:, :512] = wg_out[0]
    wgrad_ref[:, 512:] = wg_out[1]

    grp_sent(s_pl, pl_s, pl_r)
    grp_sent(s_rows, rows_s, rows_r)
    grp_sent(s_cot, cot_s, cot_r)
    sent(adj.at[mi], a_s.at[0], a_r.at[0])
    each(4, lambda q: sent(adj.at[mi], a_s.at[q], a_r.at[q]))
    each(4, lambda q: sent(adj.at[y_from(q)], f_s.at[q], f_r.at[q]))
    each(4, lambda q: sent(whole_w.at[core, mg * 4 + my_y], w1_s.at[q], w1_r.at[q]))
    each(NG, lambda p: sent(whole_w.at[core, pl.ds(mg * 4, 4)], w2_s.at[p], w2_r.at[p]))
    w3.wait_send()
    ms.wait_send()
    in_sent(lambda i: v_all.at[mi], v_s, v_r)
    in_sent(lambda i: q_rows.at[i], x_s, x_r)
    in_sent(lambda i: q_cot.at[i], c_s, c_r)
    in_sent(lambda i: mixed.at[i], m_s, m_r)
    in_sent(lambda i: gf_out.at[i], gf_s, gf_r)
    in_sent(lambda i: g_half.at[0], g_s, g_r)
    in_sent(lambda i: o_slots.at[i], o1_s, o1_r)
    in_sent(lambda i: z_slots.at[i], z1_s, z1_r)
    grp_sent(o_send, o2_s, o2_r)
    grp_sent(z_send, z2_s, z2_r)
    grp_sent(wg, rs_s, rs_r)
    for h in range(2):
        @pl.when(jnp.logical_not(jnp.logical_and(t_self, core == h)))
        def _():
            sent(wg_sum.at[h], t_s.at[h], t_r.at[core])


def scratch():
    v = pltpu.VMEM
    dma = pltpu.SemaphoreType.DMA
    grp_rows = v((NG, 16, D), BF)
    bufs = [
        grp_rows, grp_rows, v((NG, 16, ROWS), BF), v((NG, 16, ROWS), BF), grp_rows, grp_rows,
        v((8, D), F32), v((8, D), F32), v((2, 64, 16, 512), BF), v((NI, ROWS, D), BF),
        v((NI, NI, 32, 128), BF), v((NI, NI, 32, 128), BF), v((NI, 16, SLOTS), BF),
        v((NI, 32, D), BF), v((NI, 32, D), BF), v((NI, ROWS, SLOTS), BF),
        v((NI, ROWS, 128), BF), v((NI, ROWS, 128), BF), v((ROWS, D), BF),
        v((2, ROWS, 512), BF), v((NI, ROWS, 512), BF), v((NI, ROWS, 128), BF), v((NI, ROWS, 128), BF),
        v((NI, 32, D), BF), v((NI, 32, D), BF), grp_rows, grp_rows,
        v((NI, NI, 32, 128), BF), v((NI, NI, 32, 128), BF), grp_rows, grp_rows,
        v((NG, 16, 512), F32), v((NG, 16, 512), F32), v((2, 8, 512), F32), v((2, 8, 512), F32),
    ]
    g, i, y, one, two = dma((NG,)), dma((NI,)), dma((4,)), dma, dma((2,))
    sems = []
    for s in [g, g, g, one, y, g, one, y, y, i, i, i, i, one, i, i, i, g, i, g, g, two]:
        sems += [s, s]
    return bufs + sems


def per_device(
    encoded, owner_slot, label_mask, cotangent, weight, block_cols, block_counts, block_values
):
    vm = pl.BlockSpec(memory_space=pltpu.VMEM)
    sm = pl.BlockSpec(memory_space=pltpu.SMEM)
    return tuple(pl.pallas_call(
        kernel,
        out_shape=(
            jax.ShapeDtypeStruct((ROWS, D), BF),
            jax.ShapeDtypeStruct((ROWS, D), BF),
            jax.ShapeDtypeStruct((8, D), F32),
        ),
        in_specs=[sm, sm, vm, vm, vm, vm, vm, vm],
        out_specs=(vm, vm, vm),
        scratch_shapes=scratch(),
        compiler_params=pltpu.CompilerParams(
            collective_id=0, has_side_effects=True, vmem_limit_bytes=48 * 1024 * 1024
        ),
    )(
        block_cols, block_counts, encoded, owner_slot.reshape(1, ROWS),
        label_mask.reshape(1, ROWS), cotangent, weight, block_values[0],
    ))


def solution(mesh):
    rows = P(("grp", "in"), None)
    flat = P(("grp", "in"))
    in_specs = (rows, flat, flat, rows, rows, rows, flat, P(("grp", "in"), None, None, None))
    return jax.shard_map(
        per_device, mesh=mesh, in_specs=in_specs, out_specs=(rows, rows, rows), check_vma=False
    )
```

```python
import functools

import jax
import jax.numpy as jnp
from jax import lax
from jax.experimental import pallas as pl
from jax.experimental.pallas import tpu as pltpu
from jax.sharding import PartitionSpec as P

MESH = pl.DeviceIdType.MESH
BF = jnp.bfloat16
F32 = jnp.float32
I32 = jnp.int32

NG = 16
NI = 8
ROWS = 128
D = 1024
SLOTS = 256


def iota(shape, dim):
    return lax.broadcasted_iota(I32, shape, dim)


def ones_where(cond):
    return jnp.where(cond, 1.0, 0.0).astype(BF)


def dot(a, b):
    return jnp.dot(a, b, preferred_element_type=F32)


def dot_t0(a, b):
    return lax.dot_general(a, b, (((0,), (0,)), ((), ())), preferred_element_type=F32)


def dot_t1(a, b):
    return lax.dot_general(a, b, (((1,), (1,)), ((), ())), preferred_element_type=F32)


def kernel(
    cols_ref, count_ref, slot_ref, mask_ref, enc_hbm, cot_hbm, w_hbm, val_hbm,
    out_ref, grad_ref, wgrad_ref,
    enc_ref, cot_ref, w_ref, val_ref,
    s_rows, r_rows, s_pl, r_pl, s_cot, r_cot,
    w_f32, w_got, whole_w, adj_up, adj,
    q_rows, x_slots, v_all, q_cot, c_slots, place, place_t,
    mixed, mixed_pair,
    g_half, g_pair, gf_out, gf_in,
    o_slots, o_mid, o_send, o_back,
    z_slots, z_mid, z_send, z_back,
    wa, wb, wa_in, wb_in, wa_sum, wb_sum, wa_in2, wb_in2, wy, wy_in, w_fin, w_fin_in,
    load,
    rows_s, rows_r, pl_s, pl_r, cot_s, cot_r,
    w0_s, w0_r, w1_s, w1_r, w2_s, w2_r, w3_s, w3_r,
    a_s, a_r, f_s, f_r,
    x_s, x_r, v_s, v_r, c_s, c_r,
    m_s, m_r, ms_s, ms_r,
    g_s, g_r, gf_s, gf_r,
    o1_s, o1_r, o2_s, o2_r,
    z1_s, z1_r, z2_s, z2_r,
    ra_s, ra_r, rb_s, rb_r, ra2_s, ra2_r, rb2_s, rb2_r, ry_s, ry_r, rf_s, rf_r,
):
    mg = lax.axis_index("grp")
    mi = lax.axis_index("in")
    core = lax.rem(mi, 2)
    my_y = lax.div(mi, 2)
    sib = mi + 1 - 2 * core

    arriving, leaving = {}, []

    def rcopy(src, dst, ss, rs, dev):
        return pltpu.make_async_remote_copy(
            src_ref=src, dst_ref=dst, send_sem=ss, recv_sem=rs, device_id=dev, device_id_type=MESH
        )

    def each(n, body):
        def step(p, carry):
            body(p)
            return carry

        lax.fori_loop(1, n, step, 0)

    def arrives(name, ref, rs):
        arriving[name] = lambda: rcopy(ref, ref, rs, rs, (mg, sib)).wait_recv()

    def leaves(ref, ss):
        leaving.append(lambda: rcopy(ref, ref, ss, ss, (mg, sib)).wait_send())

    def wait(name):
        arriving.pop(name)()

    def grp_to(p):
        return lax.rem(mg + p, NG)

    def in_to(p):
        return lax.rem(mi + p, NI)

    def y_to(q):
        return lax.rem(mi + 2 * q, NI)

    def y_from(q):
        return lax.rem(mi + NI - 2 * q, NI)

    def to_grp(name, src, dst, ss, rs):
        def go(p):
            rcopy(src.at[grp_to(p)], dst.at[mg], ss, rs, (grp_to(p), mi)).start()

        each(NG, go)
        leaves(src.at[pl.ds(0, NG - 1)], ss)
        arrives(name, dst.at[pl.ds(0, NG - 1)], rs)

    def to_in(name, src, dst, ss, rs, left, came):
        def go(p):
            rcopy(src(in_to(p)), dst, ss, rs, (mg, in_to(p))).start()

        each(NI, go)
        leaves(left, ss)
        arrives(name, came, rs)

    my_z, my_x = lax.div(mg, 4), lax.rem(mg, 4)

    def to_four(name, axis, src, dst, ss, rs, left, came):
        for q in range(1, 4):
            if axis == "x":
                n = lax.rem(my_x + q, 4)
                dev = (my_z * 4 + n, mi)
            elif axis == "z":
                n = lax.rem(my_z + q, 4)
                dev = (n * 4 + my_x, mi)
            else:
                n = lax.rem(my_y + q, 4)
                dev = (mg, n * 2 + core)
            rcopy(src(n), dst, ss, rs, dev).start()
        leaves(left, ss)
        arrives(name, came, rs)

    def to_sib(name, src, dst, ss, rs, came=None):
        rcopy(src, dst, ss, rs, (mg, sib)).start()
        leaves(src, ss)
        arrives(name, dst if came is None else came, rs)

    barrier = pltpu.get_barrier_semaphore()

    def greet(dev):
        pl.semaphore_signal(barrier, inc=1, device_id=dev, device_id_type=MESH)

    each(NG, lambda p: greet((grp_to(p), mi)))
    each(NI, lambda p: greet((mg, in_to(p))))

    loads = [
        pltpu.make_async_copy(src, dst, load.at[n])
        for n, (src, dst) in enumerate(
            [(enc_hbm, enc_ref), (w_hbm, w_ref), (val_hbm, val_ref), (cot_hbm, cot_ref)]
        )
    ]
    for copy in loads:
        copy.start()

    def body():
        slot_row = slot_ref[...]
        eye = iota((ROWS, ROWS), 0) == iota((ROWS, ROWS), 1)
        slot_b = jnp.broadcast_to(slot_row, (ROWS, ROWS))
        slot_col = jnp.sum(jnp.where(eye, slot_b, 0), axis=1, keepdims=True)
        own_b = lax.shift_right_logical(slot_b, 7)
        own_col = lax.shift_right_logical(slot_col, 7)
        same = own_b == jnp.broadcast_to(own_col, (ROWS, ROWS))
        n_ix, m_ix = iota((ROWS, ROWS), 0), iota((ROWS, ROWS), 1)
        rank_row = jnp.sum(jnp.where(same & (n_ix < m_ix), 1, 0), axis=0, keepdims=True)
        rank_col = jnp.sum(jnp.where(same & (m_ix < n_ix), 1, 0), axis=1, keepdims=True)
        flat_row = lax.shift_right_logical(slot_row, 7) * 2 + rank_row
        flat_col = own_col * 2 + rank_col
        spread = iota((SLOTS, ROWS), 0) == jnp.broadcast_to(flat_row, (SLOTS, ROWS))
        spread_rows = ones_where(spread)
        loads[0].wait()
        s_rows[...] = dot(spread_rows, enc_ref[...]).astype(BF).reshape(NG, 16, D)

        pl.semaphore_wait(barrier, (NG - 1) + (NI - 1))
        to_grp("rows", s_rows, r_rows, rows_s, rows_r)
        r_rows[mg] = s_rows[mg]

        place1 = jnp.bitwise_and(slot_col, ROWS - 1) + 1
        place_b = jnp.broadcast_to(place1, (ROWS, ROWS)).astype(F32).astype(BF)
        s_pl[...] = dot(spread_rows, place_b).astype(BF).reshape(NG, 16, ROWS)
        to_grp("pl", s_pl, r_pl, pl_s, pl_r)
        r_pl[mg] = s_pl[mg]
        loads[1].wait()
        w_f32[...] = w_ref[...].astype(F32)
        to_sib("w0", w_f32, w_got, w0_s, w0_r)

        loads[2].wait()
        count = count_ref[0, 0]
        for j in range(5):
            col = lax.rem(mi + j, NI)
            acc = jnp.zeros((ROWS, ROWS), F32)
            for k in range(10):
                live = jnp.logical_and(cols_ref[0, k] == col, count > k)
                acc = acc + val_ref[0, k].astype(F32) * jnp.where(live, 1.0, 0.0)
            adj_up[mi, j] = acc.astype(BF)
        wait("w0")
        first = core == 0
        pair = jnp.concatenate(
            [
                jnp.where(first, w_f32[...], w_got[...]),
                jnp.where(first, w_got[...], w_f32[...]),
            ],
            axis=0,
        )
        pair = jnp.where(first, pair[:, :512], pair[:, 512:]).astype(BF)
        mine_w = whole_w.at[core, my_z, my_x, my_y]
        mine_w[...] = pair
        to_four(
            "w1", "y", lambda n: mine_w, mine_w, w1_s, w1_r,
            whole_w.at[core, 0, 0, pl.ds(0, 3)], whole_w.at[core, 0, 0, pl.ds(0, 3)],
        )

        mine_up = adj_up.at[mi]
        for q in range(1, 4):
            rcopy(mine_up, mine_up, a_s.at[q], a_r.at[q], (mg, y_to(q))).start()
            leaves(mine_up, a_s.at[q])
            arrives("a%d" % q, mine_up, a_r.at[q])
        to_sib("a0", mine_up, mine_up, a_s.at[0], a_r.at[0])


        spread_cot = ones_where(spread & (jnp.broadcast_to(mask_ref[...], (SLOTS, ROWS)) > 0))
        loads[3].wait()
        s_cot[...] = dot(spread_cot, cot_ref[...]).astype(BF).reshape(NG, 16, D)
        to_grp("cot", s_cot, r_cot, cot_s, cot_r)
        r_cot[mg] = s_cot[mg]

        collect = ones_where(
            iota((ROWS, SLOTS), 1) == jnp.broadcast_to(flat_col, (ROWS, SLOTS))
        )
        flat_out = (
            jnp.bitwise_and(own_col, 7) * 32 + lax.shift_right_logical(own_col, 3) * 2 + rank_col
        )
        collect_out = ones_where(
            iota((ROWS, SLOTS), 1) == jnp.broadcast_to(flat_out, (ROWS, SLOTS))
        )

        r_ix, c_ix = iota((SLOTS, SLOTS), 0), iota((SLOTS, SLOTS), 1)

        def moved(ix):
            return (
                lax.shift_right_logical(jnp.bitwise_and(ix, 31), 1) * 16
                + lax.shift_right_logical(ix, 5) * 2
                + jnp.bitwise_and(ix, 1)
            )

        perm = ones_where(c_ix == moved(r_ix))
        perm_t = ones_where(r_ix == moved(c_ix))
        low = (jnp.bitwise_and(r_ix, 31) == jnp.bitwise_and(c_ix, 31)) & (
            lax.shift_right_logical(c_ix, 5) == mi
        )
        o_rows = ones_where(
            iota((16, SLOTS), 0) == lax.shift_right_logical(iota((16, SLOTS), 1), 5)
        )

        wait("pl")
        pl_cols = dot(perm, r_pl[...].reshape(SLOTS, ROWS))
        pl_wide = jnp.concatenate([pl_cols, pl_cols], axis=1)
        v_all[mi] = dot(o_rows, jnp.where(low, pl_wide, 0.0).astype(BF)).astype(BF)
        seven = pl.ds(0, NI - 1)
        to_in("v", lambda i: v_all.at[mi], v_all.at[mi], v_s, v_r, v_all.at[seven], v_all.at[seven])

        three, left_w, right_w = pl.ds(0, 3), pl.ds(0, 256), pl.ds(256, 256)
        wait("w1")
        group_l = whole_w.at[core, my_z, my_x, :, :, left_w]
        group_r = whole_w.at[core, my_z, my_x, :, :, right_w]
        some = whole_w.at[core, 0, three, :, :, left_w]
        to_four("w2l", "x", lambda n: group_l, group_l, w2_s.at[0], w2_r.at[0], some, some)
        to_four("w2r", "z", lambda n: group_r, group_r, w2_s.at[1], w2_r.at[1], some, some)
        wait("rows")
        for f in range(NI):
            part = r_rows[:, :, f * 128:(f + 1) * 128].reshape(SLOTS, 128)
            q_rows[f] = dot(perm, part).astype(BF).reshape(NI, 32, 128)
        to_in(
            "x", lambda i: q_rows.at[i], x_slots.at[:, mi], x_s, x_r,
            q_rows.at[seven], x_slots.at[:, seven],
        )
        x_slots[:, mi] = q_rows[mi]

        for q in range(1, 4):
            wait("a%d" % q)
            ref = adj_up.at[y_from(q)]
            to_sib(
                "f%d" % q, ref, ref, f_s.at[q], f_r.at[q],
                adj_up.at[lax.rem(sib + NI - 2 * q, NI)],
            )
        wait("cot")
        q_cot[...] = dot(perm, r_cot[...].reshape(SLOTS, D)).astype(BF).reshape(NI, 32, D)
        to_in(
            "c", lambda i: q_cot.at[i], c_slots.at[mi], c_s, c_r, q_cot.at[seven], c_slots.at[seven]
        )
        c_slots[mi] = q_cot[mi]

        wait("w2l")
        wait("w2r")
        plane_l = whole_w.at[core, my_z, :, :, :, left_w]
        plane_r = whole_w.at[core, :, my_x, :, :, right_w]
        some = whole_w.at[core, three, :, :, :, left_w]
        to_four("w3l", "z", lambda n: plane_l, plane_l, w2_s.at[2], w2_r.at[2], some, some)
        to_four("w3r", "x", lambda n: plane_r, plane_r, w2_s.at[3], w2_r.at[3], some, some)


        wait("v")
        v_sum = v_all[0].astype(F32)
        for i in range(1, NI):
            v_sum = v_sum + v_all[i].astype(F32)
        node1 = (iota((ROWS, SLOTS), 0) + 1).astype(F32)
        for o in range(NI):
            here = jnp.where(node1 == jnp.broadcast_to(v_sum[o:o + 1, :], (ROWS, SLOTS)), 1.0, 0.0)
            place[o] = here.astype(BF)
            place_t[o] = here.T.astype(BF)

        for name in ("a0", "f1", "f2", "f3"):
            wait(name)
        for r in range(NI):
            for j in range(5):
                c = (r + j) % NI
                adj[r * 128:(r + 1) * 128, c * 128:(c + 1) * 128] = adj_up[r, j]
                if 0 < j < 4:
                    flipped = adj_up[r, j].astype(F32).T.astype(BF)
                    adj[c * 128:(c + 1) * 128, r * 128:(r + 1) * 128] = flipped

        wait("x")
        feats = jnp.concatenate(
            [dot(place[o], x_slots[o].reshape(SLOTS, 128)).astype(BF) for o in range(NI)], axis=0
        )
        mixed[...] = dot(adj[...], feats).astype(BF).reshape(NI, ROWS, 128)
        my_rows = mixed_pair.at[0]
        my_cols = pl.ds(pl.multiple_of(mi * 128, 128), 128)
        to_in(
            "m", lambda i: mixed.at[i], my_rows.at[:, my_cols], m_s, m_r,
            mixed.at[seven], my_rows.at[:, pl.ds(0, 7 * 128)],
        )
        my_rows[:, my_cols] = mixed[mi]

        wait("w3l")
        wait("w3r")
        to_sib("w3", whole_w.at[core], whole_w.at[core], w3_s, w3_r, whole_w.at[1 - core])

        wait("c")
        place_out = dot(place[mi], perm).astype(BF)
        own_cot = dot(place[mi], c_slots[...].reshape(SLOTS, D))

        wait("w3")
        wait("m")
        to_sib("ms", my_rows, mixed_pair.at[1], ms_s, ms_r)
        rows_val = mixed_pair[0]
        for h in range(2):
            v = dot(rows_val, whole_w[h].reshape(D, 512))
            k0 = 0.7978845608028654
            th = jnp.tanh(k0 * (v + 0.044715 * (v * v * v)))
            act = 0.5 * v * (1.0 + th)
            slope = 0.5 * (1.0 + th) + 0.5 * v * (1.0 - th * th) * (k0 * (1.0 + 3 * 0.044715 * (v * v)))
            g_half[h] = (own_cot[:, h * 512:(h + 1) * 512] * slope).astype(BF)
            out_ref[:, h * 512:(h + 1) * 512] = act.astype(BF)

        to_sib("g", g_half.at[1 - core], g_pair.at[1], g_s, g_r)
        g_pair[0] = g_half[core]

        for f in range(NI):
            w_rows = whole_w[:, f // 2, f % 2 * 2:f % 2 * 2 + 2]
            gf_out[f] = (
                dot_t1(g_half[0], w_rows[0].reshape(128, 512))
                + dot_t1(g_half[1], w_rows[1].reshape(128, 512))
            ).astype(BF)
        to_in("gf", lambda i: gf_out.at[i], gf_in.at[mi], gf_s, gf_r, gf_out.at[seven], gf_in.at[seven])
        gf_in[mi] = gf_out[mi]

        o_slots[...] = dot_t0(place_out, out_ref[...]).astype(BF).reshape(NG, 16, D)
        to_grp("o1", o_slots, o_mid, o1_s, o1_r)
        o_mid[mg] = o_slots[mg]

        wait("ms")
        wait("g")
        m_val = mixed_pair[...].reshape(2 * ROWS, D)
        for h in range(2):
            term = dot_t0(m_val, g_pair[:, :, h * 256:(h + 1) * 256].reshape(2 * ROWS, 256))
            term = term.astype(BF).reshape(4, 4, 64, 256)
            for n in range(4):
                if h == 0:
                    wa[n] = term[:, n]
                else:
                    wb[n] = term[n]
        to_four("ra", "x", lambda n: wa.at[n], wa_in.at[my_x], ra_s, ra_r, wa.at[three], wa.at[three])
        to_four("rb", "z", lambda n: wb.at[n], wb_in.at[my_z], rb_s, rb_r, wb.at[three], wb.at[three])
        wa_in[my_x] = wa[my_x]
        wb_in[my_z] = wb[my_z]

        wait("gf")
        feed = gf_in[...].reshape(D, 128)
        back = dot(adj[...], feed).astype(BF)
        for o in range(NI):
            z_slots[:, o] = (
                dot(place_t[o], back[o * 128:(o + 1) * 128]).astype(BF).reshape(NI, 32, 128)
            )
        to_in("z1", lambda i: z_slots.at[i], z_mid.at[mi], z1_s, z1_r, z_slots.at[seven], z_mid.at[seven])
        z_mid[mi] = z_slots[mi]

        def add(ref):
            out = ref[0].astype(F32)
            for n in range(1, 4):
                out = out + ref[n].astype(F32)
            return out

        wait("ra")
        wa_sum[...] = add(wa_in).astype(BF)
        wait("rb")
        wb_sum[...] = add(wb_in).astype(BF)
        part = wa_sum.at[three]
        to_four("ra2", "z", lambda n: wa_sum.at[n], wa_in2.at[my_z], ra2_s, ra2_r, part, part)
        to_four("rb2", "x", lambda n: wb_sum.at[n], wb_in2.at[my_x], rb2_s, rb2_r, part, part)
        wa_in2[my_z] = wa_sum[my_z]
        wb_in2[my_x] = wb_sum[my_x]

        wait("z1")
        for f in range(NI):
            z_send[:, :, f * 128:(f + 1) * 128] = (
                dot(perm_t, z_mid[f].reshape(SLOTS, 128)).astype(BF).reshape(NG, 16, 128)
            )
        to_grp("z2", z_send, z_back, z2_s, z2_r)
        z_back[mg] = z_send[mg]

        wait("o1")
        o_send[...] = dot(perm, o_mid[...].reshape(SLOTS, D)).astype(BF).reshape(NI, 32, D)
        to_in("o2", lambda i: o_send.at[i], o_back.at[mi], o2_s, o2_r, o_send.at[seven], o_back.at[seven])
        o_back[mi] = o_send[mi]

        wait("ra2")
        wait("rb2")
        wy[:, :, :256] = add(wa_in2).reshape(4, 16, 256)
        wy[:, :, 256:] = add(wb_in2).reshape(4, 16, 256)
        to_four("ry", "y", lambda n: wy.at[n], wy_in.at[my_y], ry_s, ry_r, wy.at[three], wy.at[three])
        wy_in[my_y] = wy[my_y]
        wait("o2")
        out_ref[...] = dot(collect_out, o_back[...].reshape(SLOTS, D)).astype(BF)
        wait("ry")
        w_fin[...] = (add(wy_in) * (1.0 / 128)).reshape(2, 8, 512)
        to_sib("rf", w_fin.at[1 - core], w_fin_in, rf_s, rf_r)
        wgrad_ref[:, pl.ds(pl.multiple_of(core * 512, 512), 512)] = w_fin[core]
        wait("z2")
        grad_ref[...] = dot(collect, z_back[...].reshape(SLOTS, D)).astype(BF)
        wait("rf")
        wgrad_ref[:, pl.ds(pl.multiple_of((1 - core) * 512, 512), 512)] = w_fin_in[...]

    body()
    for name in list(arriving):
        wait(name)
    for done in leaving:
        done()


def store(a, b, c, a_out, b_out, c_out):
    a_out[...] = a[...]
    b_out[...] = b[...]
    c_out[...] = c[...]


def scratch():
    v = pltpu.VMEM
    dma = pltpu.SemaphoreType.DMA
    big, small = v((4, 4, 64, 256), BF), v((4, 64, 256), BF)
    grp_rows = v((NG, 16, D), BF)
    bufs = [
        v((ROWS, D), BF), v((ROWS, D), BF), v((8, D), BF), v((1, 10, ROWS, ROWS), BF),
        grp_rows, grp_rows, v((NG, 16, ROWS), BF), v((NG, 16, ROWS), BF), grp_rows, grp_rows,
        v((8, D), F32), v((8, D), F32), v((2, 4, 4, 4, 16, 512), BF), v((NI, 5, ROWS, ROWS), BF),
        v((D, D), BF),
        v((NI, NI, 32, 128), BF), v((NI, NI, 32, 128), BF), v((NI, 16, SLOTS), BF),
        v((NI, 32, D), BF), v((NI, 32, D), BF), v((NI, ROWS, SLOTS), BF), v((NI, SLOTS, ROWS), BF),
        v((NI, ROWS, 128), BF), v((2, ROWS, D), BF),
        v((2, ROWS, 512), BF), v((2, ROWS, 512), BF), v((NI, ROWS, 128), BF), v((NI, ROWS, 128), BF),
        grp_rows, grp_rows, v((NI, 32, D), BF), v((NI, 32, D), BF),
        v((NI, NI, 32, 128), BF), v((NI, NI, 32, 128), BF), grp_rows, grp_rows,
        big, big, big, big, small, small, small, small, v((4, 16, 512), F32), v((4, 16, 512), F32),
        v((2, 8, 512), F32), v((8, 512), F32),
    ]
    one, four = dma, dma((4,))
    sems = [four]
    for s in [one] * 5 + [four] + [one] + [four] * 2 + [one] * 17:
        sems += [s, s]
    return bufs + sems


def per_device(
    encoded, owner_slot, label_mask, cotangent, weight, block_cols, block_counts, block_values
):
    vm = pl.BlockSpec(memory_space=pltpu.VMEM)
    sm = pl.BlockSpec(memory_space=pltpu.SMEM)
    results = pl.pallas_call(
        kernel,
        out_shape=(
            jax.ShapeDtypeStruct((ROWS, D), BF),
            jax.ShapeDtypeStruct((ROWS, D), BF),
            jax.ShapeDtypeStruct((8, D), F32),
        ),
        in_specs=[sm, sm, vm, vm] + [pl.BlockSpec(memory_space=pl.ANY)] * 4,
        out_specs=(vm, vm, vm),
        scratch_shapes=scratch(),
        compiler_params=pltpu.CompilerParams(
            collective_id=0, has_side_effects=True, vmem_limit_bytes=60 * 1024 * 1024
        ),
    )(
        block_cols, block_counts.reshape(1, 1), owner_slot.reshape(1, ROWS), label_mask.reshape(1, ROWS),
        encoded, cotangent, weight, block_values,
    )
    return tuple(pl.pallas_call(
        store,
        out_shape=tuple(jax.ShapeDtypeStruct(r.shape, r.dtype) for r in results),
        in_specs=[vm] * 3,
        out_specs=(vm,) * 3,
    )(*results))


def solution(mesh):
    rows = P(("grp", "in"), None)
    flat = P(("grp", "in"))
    in_specs = (rows, flat, flat, rows, rows, rows, flat, P(("grp", "in"), None, None, None))
    return jax.shard_map(
        per_device, mesh=mesh, in_specs=in_specs, out_specs=(rows, rows, rows), check_vma=False
    )
```

```python
import functools

import jax
import jax.numpy as jnp
from jax import lax
from jax.experimental import pallas as pl
from jax.experimental.pallas import tpu as pltpu
from jax.sharding import PartitionSpec as P

MESH = pl.DeviceIdType.MESH
BF = jnp.bfloat16
F32 = jnp.float32
I32 = jnp.int32

NG = 16
NI = 8
ROWS = 128
D = 1024
SLOTS = 256


def iota(shape, dim):
    return lax.broadcasted_iota(I32, shape, dim)


def ones_where(cond):
    return jnp.where(cond, 1.0, 0.0).astype(BF)


def dot(a, b):
    return jnp.dot(a, b, preferred_element_type=F32)


def dot_t0(a, b):
    return lax.dot_general(a, b, (((0,), (0,)), ((), ())), preferred_element_type=F32)


def dot_t1(a, b):
    return lax.dot_general(a, b, (((1,), (1,)), ((), ())), preferred_element_type=F32)


def kernel(
    cols_hbm, slot_hbm, mask_hbm, count_hbm, enc_hbm, cot_hbm, w_hbm, val_hbm,
    out_hbm, grad_hbm, wgrad_hbm,
    out_ref, grad_ref, wgrad_ref, cols_ref, slot_ref, mask_ref, count_ref, enc_ref, cot_ref, w_ref, val_ref,
    s_rows, r_rows, s_pl, r_pl, s_cot, r_cot,
    w_f32, w_got, whole_w, adj_up, adj,
    q_rows, x_slots, v_all, q_cot, c_slots, place, place_t,
    mixed, mixed_pair,
    g_half, g_pair, gf_out, gf_in,
    o_slots, o_mid, o_send, o_back,
    z_slots, z_mid, z_send, z_back,
    wa, wb, wa_in, wb_in, wa_sum, wb_sum, wa_in2, wb_in2, wy, wy_in,
    load, store,
    rows_s, rows_r, pl_s, pl_r, cot_s, cot_r,
    w0_s, w0_r, w1_s, w1_r, w2_s, w2_r, w3_s, w3_r,
    a_s, a_r, f_s, f_r,
    x_s, x_r, v_s, v_r, c_s, c_r,
    m_s, m_r, ms_s, ms_r,
    g_s, g_r, gf_s, gf_r,
    o1_s, o1_r, o2_s, o2_r,
    z1_s, z1_r, z2_s, z2_r,
    ra_s, ra_r, rb_s, rb_r, ra2_s, ra2_r, rb2_s, rb2_r, ry_s, ry_r,
):
    mg = lax.axis_index("grp")
    mi = lax.axis_index("in")
    core = lax.rem(mi, 2)
    my_y = lax.div(mi, 2)
    sib = mi + 1 - 2 * core

    arriving, leaving = {}, []

    def rcopy(src, dst, ss, rs, dev):
        return pltpu.make_async_remote_copy(
            src_ref=src, dst_ref=dst, send_sem=ss, recv_sem=rs, device_id=dev, device_id_type=MESH
        )

    def each(n, body):
        def step(p, carry):
            body(p)
            return carry

        lax.fori_loop(1, n, step, 0)

    def arrives(name, ref, rs):
        arriving[name] = lambda: rcopy(ref, ref, rs, rs, (mg, sib)).wait_recv()

    def leaves(ref, ss):
        leaving.append(lambda: rcopy(ref, ref, ss, ss, (mg, sib)).wait_send())

    def wait(name):
        arriving.pop(name)()

    def grp_to(p):
        return lax.rem(mg + 7 * p, NG)

    def in_to(p):
        return lax.rem(mi + 3 * p, NI)

    def y_to(q):
        return lax.rem(mi + 2 * q, NI)

    def y_from(q):
        return lax.rem(mi + NI - 2 * q, NI)

    def to_grp(name, src, dst, ss, rs):
        def go(p):
            rcopy(src.at[grp_to(p)], dst.at[mg], ss, rs, (grp_to(p), mi)).start()

        each(NG, go)
        leaves(src.at[pl.ds(0, NG - 1)], ss)
        arrives(name, dst.at[pl.ds(0, NG - 1)], rs)

    def to_in(name, src, dst, ss, rs, left, came):
        def go(p):
            rcopy(src(in_to(p)), dst, ss, rs, (mg, in_to(p))).start()

        each(NI, go)
        leaves(left, ss)
        arrives(name, came, rs)

    my_z, my_x = lax.div(mg, 4), lax.rem(mg, 4)
    my_gz = lax.div(my_z, 2) * 4 + my_x

    def to_four(name, axis, src, dst, ss, rs, left, came):
        for q in range(1, 4):
            if axis == "x":
                n = lax.rem(my_x + q, 4)
                dev = (my_z * 4 + n, mi)
            elif axis == "z":
                n = lax.rem(my_z + q, 4)
                dev = (n * 4 + my_x, mi)
            else:
                n = lax.rem(my_y + q, 4)
                dev = (mg, n * 2 + core)
            rcopy(src(n), dst, ss, rs, dev).start()
        leaves(left, ss)
        arrives(name, came, rs)

    def to_sib(name, src, dst, ss, rs, came=None):
        rcopy(src, dst, ss, rs, (mg, sib)).start()
        leaves(src, ss)
        arrives(name, dst if came is None else came, rs)

    loads = [
        pltpu.make_async_copy(src, dst, load.at[n])
        for n, (src, dst) in enumerate(
            [(enc_hbm, enc_ref), (w_hbm, w_ref), (val_hbm, val_ref), (cot_hbm, cot_ref), (count_hbm, count_ref),
             (cols_hbm, cols_ref), (slot_hbm, slot_ref), (mask_hbm, mask_ref)]
        )
    ]
    for n in (6, 0, 1, 2, 4, 5, 7, 3):
        loads[n].start()

    seven = pl.ds(0, NI - 1)

    barrier = pltpu.get_barrier_semaphore()

    def greet(dev):
        pl.semaphore_signal(barrier, inc=1, device_id=dev, device_id_type=MESH)

    each(NG, lambda p: greet((grp_to(p), mi)))
    each(NI, lambda p: greet((mg, in_to(p))))

    stores = [
        pltpu.make_async_copy(src, dst, store.at[n])
        for n, (src, dst) in enumerate(
            [(out_ref, out_hbm), (grad_ref, grad_hbm), (wgrad_ref, wgrad_hbm)]
        )
    ]

    def body():
        loads[6].wait()
        slot_row = slot_ref[...]
        eye = iota((ROWS, ROWS), 0) == iota((ROWS, ROWS), 1)
        slot_b = jnp.broadcast_to(slot_row, (ROWS, ROWS))
        slot_col = jnp.sum(jnp.where(eye, slot_b, 0), axis=1, keepdims=True)
        own_b = lax.shift_right_logical(slot_b, 7)
        own_col = lax.shift_right_logical(slot_col, 7)
        same = own_b == jnp.broadcast_to(own_col, (ROWS, ROWS))
        n_ix, m_ix = iota((ROWS, ROWS), 0), iota((ROWS, ROWS), 1)
        rank_row = jnp.sum(jnp.where(same & (n_ix < m_ix), 1, 0), axis=0, keepdims=True)
        rank_col = jnp.sum(jnp.where(same & (m_ix < n_ix), 1, 0), axis=1, keepdims=True)
        flat_row = lax.shift_right_logical(slot_row, 7) * 2 + rank_row
        flat_col = own_col * 2 + rank_col
        spread = iota((SLOTS, ROWS), 0) == jnp.broadcast_to(flat_row, (SLOTS, ROWS))
        spread_rows = ones_where(spread)
        place1 = jnp.bitwise_and(slot_col, ROWS - 1) + 1
        place_b = jnp.broadcast_to(place1, (ROWS, ROWS)).astype(F32).astype(BF)
        s_pl[...] = dot(spread_rows, place_b).astype(BF).reshape(NG, 16, ROWS)
        loads[0].wait()
        s_rows[...] = dot(spread_rows, enc_ref[...]).astype(BF).reshape(NG, 16, D)

        pl.semaphore_wait(barrier, (NG - 1) + (NI - 1))
        to_grp("pl", s_pl, r_pl, pl_s, pl_r)
        to_grp("rows", s_rows, r_rows, rows_s, rows_r)
        r_rows[mg] = s_rows[mg]

        r_pl[mg] = s_pl[mg]
        loads[1].wait()
        w_f32[...] = w_ref[...].astype(F32)
        to_sib("w0", w_f32, w_got, w0_s, w0_r)

        loads[2].wait()
        loads[4].wait()
        loads[5].wait()
        count = count_ref[0]
        for j in range(5):
            col = lax.rem(mi + j, NI)
            acc = jnp.zeros((ROWS, ROWS), F32)
            for k in range(10):
                live = jnp.logical_and(cols_ref[0, k] == col, count > k)
                acc = acc + val_ref[0, k].astype(F32) * jnp.where(live, 1.0, 0.0)
            adj_up[mi, j] = acc.astype(BF)
        wait("w0")
        first = core == 0
        pair = jnp.concatenate(
            [
                jnp.where(first, w_f32[...], w_got[...]),
                jnp.where(first, w_got[...], w_f32[...]),
            ],
            axis=0,
        )
        pair = jnp.where(first, pair[:, :512], pair[:, 512:]).astype(BF)
        mine_w = whole_w.at[core, my_z, my_x, my_y]
        mine_w[...] = pair
        to_four(
            "w1", "y", lambda n: mine_w, mine_w, w1_s, w1_r,
            whole_w.at[core, 0, 0, pl.ds(0, 3)], whole_w.at[core, 0, 0, pl.ds(0, 3)],
        )

        mine_up = adj_up.at[mi]
        for q in (1, 3):
            rcopy(mine_up, mine_up, a_s.at[q], a_r.at[q], (mg, y_to(q))).start()
            leaves(mine_up, a_s.at[q])
            arrives("a%d" % q, mine_up, a_r.at[q])
        to_sib("a0", mine_up, mine_up, a_s.at[0], a_r.at[0])


        loads[7].wait()
        spread_cot = ones_where(spread & (jnp.broadcast_to(mask_ref[...], (SLOTS, ROWS)) > 0))
        loads[3].wait()
        s_cot[...] = dot(spread_cot, cot_ref[...]).astype(BF).reshape(NG, 16, D)
        to_grp("cot", s_cot, r_cot, cot_s, cot_r)
        r_cot[mg] = s_cot[mg]

        collect = ones_where(
            iota((ROWS, SLOTS), 1) == jnp.broadcast_to(flat_col, (ROWS, SLOTS))
        )
        own_g = lax.shift_right_logical(own_col, 3)
        even_first = (
            jnp.bitwise_and(own_g, 4) * 2
            + lax.shift_right_logical(jnp.bitwise_and(own_g, 8), 1)
            + jnp.bitwise_and(own_g, 3)
        )
        flat_out = jnp.bitwise_and(own_col, 7) * 32 + even_first * 2 + rank_col
        collect_out = ones_where(
            iota((ROWS, SLOTS), 1) == jnp.broadcast_to(flat_out, (ROWS, SLOTS))
        )

        r_ix, c_ix = iota((SLOTS, SLOTS), 0), iota((SLOTS, SLOTS), 1)

        def moved(ix):
            z = jnp.bitwise_and(lax.shift_right_logical(ix, 2), 2) + jnp.bitwise_and(
                lax.shift_right_logical(ix, 4), 1
            )
            x = jnp.bitwise_and(lax.shift_right_logical(ix, 1), 3)
            return (
                (z * 4 + x) * 16 + lax.shift_right_logical(ix, 5) * 2 + jnp.bitwise_and(ix, 1)
            )

        perm = ones_where(c_ix == moved(r_ix))
        perm_t = ones_where(r_ix == moved(c_ix))
        low = (jnp.bitwise_and(r_ix, 31) == jnp.bitwise_and(c_ix, 31)) & (
            lax.shift_right_logical(c_ix, 5) == mi
        )
        o_rows = ones_where(
            iota((16, SLOTS), 0) == lax.shift_right_logical(iota((16, SLOTS), 1), 5)
        )

        wait("pl")
        pl_cols = dot(perm, r_pl[...].reshape(SLOTS, ROWS))
        pl_wide = jnp.concatenate([pl_cols, pl_cols], axis=1)
        v_all[mi] = dot(o_rows, jnp.where(low, pl_wide, 0.0).astype(BF)).astype(BF)
        to_in("v", lambda i: v_all.at[mi], v_all.at[mi], v_s, v_r, v_all.at[seven], v_all.at[seven])

        three, left_w, right_w = pl.ds(0, 3), pl.ds(0, 256), pl.ds(256, 256)
        wait("w1")
        group_l = whole_w.at[core, my_z, my_x, :, :, left_w]
        group_r = whole_w.at[core, my_z, my_x, :, :, right_w]
        some = whole_w.at[core, 0, three, :, :, left_w]
        to_four("w2l", "x", lambda n: group_l, group_l, w2_s.at[0], w2_r.at[0], some, some)
        to_four("w2r", "z", lambda n: group_r, group_r, w2_s.at[1], w2_r.at[1], some, some)

        for q, h in ((1, 2), (3, 4)):
            wait("a%d" % q)
            ref = adj_up.at[y_from(q), :, pl.ds(0 if q == 1 else 64, 64)]
            rcopy(ref, ref, a_s.at[h], a_r.at[h], (mg, y_to(q))).start()
            leaves(ref, a_s.at[h])
            arrives("a%d" % h, ref, a_r.at[h])
        wait("rows")
        for f in range(NI):
            part = r_rows[:, :, f * 128:(f + 1) * 128].reshape(SLOTS, 128)
            q_rows[f] = dot(perm, part).astype(BF).reshape(NI, 32, 128)
        to_in(
            "x", lambda i: q_rows.at[i], x_slots.at[:, mi], x_s, x_r,
            q_rows.at[seven], x_slots.at[:, seven],
        )
        x_slots[:, mi] = q_rows[mi]

        wait("a2")
        wait("a4")
        for q in range(1, 4):
            ref = adj_up.at[y_from(q)]
            to_sib(
                "f%d" % q, ref, ref, f_s.at[q], f_r.at[q],
                adj_up.at[lax.rem(sib + NI - 2 * q, NI)],
            )
        wait("cot")
        q_cot[...] = dot(perm, r_cot[...].reshape(SLOTS, D)).astype(BF).reshape(NI, 32, D)
        to_in(
            "c", lambda i: q_cot.at[i], c_slots.at[mi], c_s, c_r, q_cot.at[seven], c_slots.at[seven]
        )
        c_slots[mi] = q_cot[mi]

        wait("w2l")
        wait("w2r")
        plane_l = whole_w.at[core, my_z, :, :, :, left_w]
        plane_r = whole_w.at[core, :, my_x, :, :, right_w]
        some = whole_w.at[core, three, :, :, :, left_w]
        to_four("w3l", "z", lambda n: plane_l, plane_l, w2_s.at[2], w2_r.at[2], some, some)
        to_four("w3r", "x", lambda n: plane_r, plane_r, w2_s.at[3], w2_r.at[3], some, some)


        wait("v")
        v_sum = v_all[0].astype(F32)
        for i in range(1, NI):
            v_sum = v_sum + v_all[i].astype(F32)
        node1 = (iota((ROWS, SLOTS), 0) + 1).astype(F32)
        for o in range(NI):
            here = jnp.where(node1 == jnp.broadcast_to(v_sum[o:o + 1, :], (ROWS, SLOTS)), 1.0, 0.0)
            place[o] = here.astype(BF)
            place_t[o] = here.T.astype(BF)

        for name in ("a0", "f1", "f2", "f3"):
            wait(name)
        for r in range(NI):
            for j in range(5):
                c = (r + j) % NI
                adj[r * 128:(r + 1) * 128, c * 128:(c + 1) * 128] = adj_up[r, j]
                if 0 < j < 4:
                    flipped = adj_up[r, j].astype(F32).T.astype(BF)
                    adj[c * 128:(c + 1) * 128, r * 128:(r + 1) * 128] = flipped

        wait("x")
        feats = jnp.concatenate(
            [dot(place[o], x_slots[o].reshape(SLOTS, 128)).astype(BF) for o in range(NI)], axis=0
        )
        mixed[...] = dot(adj[...], feats).astype(BF).reshape(NI, ROWS, 128)
        my_rows = mixed_pair.at[0]
        my_cols = pl.ds(pl.multiple_of(mi * 128, 128), 128)
        to_in(
            "m", lambda i: mixed.at[i], my_rows.at[:, my_cols], m_s, m_r,
            mixed.at[seven], my_rows.at[:, pl.ds(0, 7 * 128)],
        )
        my_rows[:, my_cols] = mixed[mi]

        wait("w3l")
        wait("w3r")
        to_sib("w3", whole_w.at[core], whole_w.at[core], w3_s, w3_r, whole_w.at[1 - core])

        wait("c")
        place_out = dot(place[mi], perm).astype(BF)
        own_cot = dot(place[mi], c_slots[...].reshape(SLOTS, D))

        wait("w3")
        wait("m")
        to_sib("ms", my_rows, mixed_pair.at[1], ms_s, ms_r)
        rows_val = mixed_pair[0]
        for h in range(2):
            v = dot(rows_val, whole_w[h].reshape(D, 512))
            k0 = 0.7978845608028654
            th = jnp.tanh(k0 * (v + 0.044715 * (v * v * v)))
            act = 0.5 * v * (1.0 + th)
            slope = 0.5 * (1.0 + th) + 0.5 * v * (1.0 - th * th) * (k0 * (1.0 + 3 * 0.044715 * (v * v)))
            g_half[h] = (own_cot[:, h * 512:(h + 1) * 512] * slope).astype(BF)
            out_ref[:, h * 512:(h + 1) * 512] = act.astype(BF)

        to_sib("g", g_half.at[1 - core], g_pair.at[1], g_s, g_r)
        g_pair[0] = g_half[core]

        for f in range(NI):
            w_rows = whole_w[:, f // 2, f % 2 * 2:f % 2 * 2 + 2]
            gf_out[f] = (
                dot_t1(g_half[0], w_rows[0].reshape(128, 512))
                + dot_t1(g_half[1], w_rows[1].reshape(128, 512))
            ).astype(BF)
        to_in("gf", lambda i: gf_out.at[i], gf_in.at[mi], gf_s, gf_r, gf_out.at[seven], gf_in.at[seven])
        gf_in[mi] = gf_out[mi]

        o_slots[...] = dot_t0(place_out, out_ref[...]).astype(BF).reshape(NG, 16, D)
        to_grp("o1", o_slots, o_mid, o1_s, o1_r)
        o_mid[mg] = o_slots[mg]

        wait("ms")
        wait("g")
        m_val = mixed_pair[...].reshape(2 * ROWS, D)
        for h in range(2):
            term = dot_t0(m_val, g_pair[:, :, h * 256:(h + 1) * 256].reshape(2 * ROWS, 256))
            term = term.astype(BF).reshape(4, 4, 64, 256)
            for n in range(4):
                if h == 0:
                    wa[n] = term[:, n]
                else:
                    wb[n] = term[n]
        to_four("ra", "x", lambda n: wa.at[n], wa_in.at[my_x], ra_s, ra_r, wa.at[three], wa.at[three])
        to_four("rb", "z", lambda n: wb.at[n], wb_in.at[my_z], rb_s, rb_r, wb.at[three], wb.at[three])
        wa_in[my_x] = wa[my_x]
        wb_in[my_z] = wb[my_z]

        wait("gf")
        feed = gf_in[...].reshape(D, 128)
        back = dot(adj[...], feed).astype(BF)
        for o in range(NI):
            z_slots[:, o] = (
                dot(place_t[o], back[o * 128:(o + 1) * 128]).astype(BF).reshape(NI, 32, 128)
            )
        for h in range(2):
            rows_h = pl.ds(h * 16, 16)
            to_in(
                "z1%d" % h, lambda i: z_slots.at[i, :, rows_h], z_mid.at[mi, :, rows_h],
                z1_s.at[h], z1_r.at[h], z_slots.at[seven, :, rows_h], z_mid.at[seven, :, rows_h],
            )
        z_mid[mi] = z_slots[mi]


        def add(ref):
            out = ref[0].astype(F32)
            for n in range(1, 4):
                out = out + ref[n].astype(F32)
            return out

        wait("o1")
        o_send[...] = dot(perm, o_mid[...].reshape(SLOTS, D)).astype(BF).reshape(NI, 32, D)
        to_in("o2", lambda i: o_send.at[i], o_back.at[mi], o2_s, o2_r, o_send.at[seven], o_back.at[seven])
        o_back[mi] = o_send[mi]

        wait("ra")
        wa_sum[...] = add(wa_in).astype(BF)
        wait("rb")
        wb_sum[...] = add(wb_in).astype(BF)
        part = wa_sum.at[three]
        to_four("ra2", "z", lambda n: wa_sum.at[n], wa_in2.at[my_z], ra2_s, ra2_r, part, part)
        to_four("rb2", "x", lambda n: wb_sum.at[n], wb_in2.at[my_x], rb2_s, rb2_r, part, part)
        wa_in2[my_z] = wa_sum[my_z]
        wb_in2[my_x] = wb_sum[my_x]

        pz_r, pz_c = iota((ROWS, ROWS), 0), iota((ROWS, ROWS), 1)
        perm_z = ones_where(
            pz_c == jnp.bitwise_and(lax.shift_right_logical(pz_r, 1), 7) * 16
            + lax.shift_right_logical(pz_r, 4) * 2 + jnp.bitwise_and(pz_r, 1)
        )
        for h in range(2):
            wait("z1%d" % h)
            for f in range(NI):
                z_send[h * 8:(h + 1) * 8, :, f * 128:(f + 1) * 128] = (
                    dot(perm_z, z_mid[f, :, h * 16:(h + 1) * 16].reshape(ROWS, 128))
                    .astype(BF).reshape(8, 16, 128)
                )

            def go(p, carry):
                n = jnp.bitwise_and(my_gz + p, 7)
                dest = lax.div(n, 4) * 8 + h * 4 + lax.rem(n, 4)

                @pl.when(dest != mg)
                def _():
                    rcopy(z_send.at[h * 8 + n], z_back.at[mg], z2_s, z2_r, (dest, mi)).start()

                return carry

            lax.fori_loop(0, 8, go, 0)
        leaves(z_send.at[pl.ds(0, NG - 1)], z2_s)
        arrives("z2", z_back.at[pl.ds(0, NG - 1)], z2_r)
        z_back[mg] = z_send[lax.rem(my_z, 2) * 8 + my_gz]

        wait("ra2")
        wait("rb2")
        wy[:, :, :256] = add(wa_in2).reshape(NI, 8, 256)
        wy[:, :, 256:] = add(wb_in2).reshape(NI, 8, 256)
        to_in("ry", lambda i: wy.at[i], wy_in.at[mi], ry_s, ry_r, wy.at[seven], wy_in.at[seven])
        wy_in[mi] = wy[mi]
        wait("o2")
        out_ref[...] = dot(collect_out, o_back[...].reshape(SLOTS, D)).astype(BF)
        stores[0].start()
        wait("ry")
        for c in range(2):
            half = wy_in[c]
            for n in range(1, 4):
                half = half + wy_in[2 * n + c]
            wgrad_ref[:, c * 512:(c + 1) * 512] = half * (1.0 / 128)
        stores[2].start()
        wait("z2")
        grad_ref[...] = dot(collect, z_back[...].reshape(SLOTS, D)).astype(BF)
        stores[1].start()

    body()
    for name in list(arriving):
        wait(name)
    for done in leaving:
        done()
    for copy in stores:
        copy.wait()


def hand_over(*refs):
    here, out, kept, load, store = refs[:3], refs[3:6], refs[6:9], refs[9], refs[10]
    loads = [pltpu.make_async_copy(here[n], kept[n], load.at[n]) for n in range(3)]
    stores = [pltpu.make_async_copy(kept[n], out[n], store.at[n]) for n in range(3)]
    for copy in loads:
        copy.start()
    for n in range(3):
        loads[n].wait()
        stores[n].start()
    for copy in stores:
        copy.wait()


def scratch():
    v = pltpu.VMEM
    dma = pltpu.SemaphoreType.DMA
    big, small = v((4, 4, 64, 256), BF), v((4, 64, 256), BF)
    grp_rows = v((NG, 16, D), BF)
    bufs = [
        v((ROWS, D), BF), v((ROWS, D), BF), v((8, D), F32), pltpu.SMEM((1, 10), I32),
        v((1, ROWS), I32), v((1, ROWS), I32), pltpu.SMEM((1,), I32), v((ROWS, D), BF), v((ROWS, D), BF), v((8, D), BF), v((1, 10, ROWS, ROWS), BF),
        grp_rows, grp_rows, v((NG, 16, ROWS), BF), v((NG, 16, ROWS), BF), grp_rows, grp_rows,
        v((8, D), F32), v((8, D), F32), v((2, 4, 4, 4, 16, 512), BF), v((NI, 5, ROWS, ROWS), BF),
        v((D, D), BF),
        v((NI, NI, 32, 128), BF), v((NI, NI, 32, 128), BF), v((NI, 16, SLOTS), BF),
        v((NI, 32, D), BF), v((NI, 32, D), BF), v((NI, ROWS, SLOTS), BF), v((NI, SLOTS, ROWS), BF),
        v((NI, ROWS, 128), BF), v((2, ROWS, D), BF),
        v((2, ROWS, 512), BF), v((2, ROWS, 512), BF), v((NI, ROWS, 128), BF), v((NI, ROWS, 128), BF),
        grp_rows, grp_rows, v((NI, 32, D), BF), v((NI, 32, D), BF),
        v((NI, NI, 32, 128), BF), v((NI, NI, 32, 128), BF), grp_rows, grp_rows,
        big, big, big, big, small, small, small, small, v((NI, 8, 512), F32), v((NI, 8, 512), F32),
    ]
    one, two, four, five = dma, dma((2,)), dma((4,)), dma((5,))
    sems = [dma((8,)), dma((3,))]
    for s in [one] * 5 + [four] + [one] + [five, four] + [one] * 9 + [two] + [one] * 6:
        sems += [s, s]
    return bufs + sems


def per_device(
    encoded, owner_slot, label_mask, cotangent, weight, block_cols, block_counts, block_values
):
    anywhere = pl.BlockSpec(memory_space=pl.ANY)
    results = pl.pallas_call(
        kernel,
        out_shape=(
            jax.ShapeDtypeStruct((ROWS, D), BF),
            jax.ShapeDtypeStruct((ROWS, D), BF),
            jax.ShapeDtypeStruct((8, D), F32),
        ),
        in_specs=[anywhere] * 8,
        out_specs=(anywhere,) * 3,
        scratch_shapes=scratch(),
        compiler_params=pltpu.CompilerParams(
            collective_id=0, has_side_effects=True, vmem_limit_bytes=60 * 1024 * 1024
        ),
    )(
        block_cols, owner_slot.reshape(1, ROWS), label_mask.reshape(1, ROWS),
        block_counts, encoded, cotangent, weight, block_values,
    )
    return tuple(pl.pallas_call(
        hand_over,
        out_shape=tuple(jax.ShapeDtypeStruct(r.shape, r.dtype) for r in results),
        in_specs=[anywhere] * 3,
        out_specs=(anywhere,) * 3,
        scratch_shapes=[pltpu.VMEM(r.shape, r.dtype) for r in results]
        + [pltpu.SemaphoreType.DMA((3,))] * 2,
    )(*results))


def solution(mesh):
    rows = P(("grp", "in"), None)
    flat = P(("grp", "in"))
    in_specs = (rows, flat, flat, rows, rows, rows, flat, P(("grp", "in"), None, None, None))
    return jax.shard_map(
        per_device, mesh=mesh, in_specs=in_specs, out_specs=(rows, rows, rows), check_vma=False
    )
```

```python
import functools

import jax
import jax.numpy as jnp
from jax import lax
from jax.experimental import pallas as pl
from jax.experimental.pallas import tpu as pltpu
from jax.sharding import PartitionSpec as P

MESH = pl.DeviceIdType.MESH
BF = jnp.bfloat16
F32 = jnp.float32
I32 = jnp.int32

NG = 16
NI = 8
ROWS = 128
D = 1024
SLOTS = 256


def iota(shape, dim):
    return lax.broadcasted_iota(I32, shape, dim)


def ones_where(cond):
    return jnp.where(cond, 1.0, 0.0).astype(BF)


def dot(a, b):
    return jnp.dot(a, b, preferred_element_type=F32)


def dot_t0(a, b):
    return lax.dot_general(a, b, (((0,), (0,)), ((), ())), preferred_element_type=F32)


def dot_t1(a, b):
    return lax.dot_general(a, b, (((1,), (1,)), ((), ())), preferred_element_type=F32)


def kernel(
    cols_hbm, slot_hbm, mask_hbm, count_hbm, enc_hbm, cot_hbm, w_hbm, val_hbm,
    out_ref, grad_ref, wgrad_ref,
    cols_ref, slot_ref, mask_ref, count_ref, enc_ref, cot_ref, w_ref, val_ref,
    s_rows, r_rows, s_pl, r_pl, s_cot, r_cot, s_cot2, r_cot2,
    w_f32, w_got, whole_w, adj_up, adj,
    q_rows, x_slots, v_all, q_cot, c_slots, q_cot2, c_slots2, place, place_t,
    mixed, mixed_pair,
    g_half, g_pair, gf_out, gf_in,
    o_slots, o_mid, o_send, o_back,
    p_slots, p_mid, p_send, p_back,
    z_slots, z_mid, z_send, z_back,
    wa, wb, wa_in, wb_in, wa_sum, wb_sum, wa_in2, wb_in2, wy, wy_in,
    load,
    rows_s, rows_r, pl_s, pl_r, cot_s, cot_r,
    w0_s, w0_r, w1_s, w1_r, w2_s, w2_r, w3_s, w3_r,
    a_s, a_r, f_s, f_r,
    x_s, x_r, v_s, v_r, c_s, c_r,
    m_s, m_r, ms_s, ms_r,
    g_s, g_r, gf_s, gf_r,
    o1_s, o1_r, o2_s, o2_r,
    z1_s, z1_r, z2_s, z2_r,
    ra_s, ra_r, rb_s, rb_r, ra2_s, ra2_r, rb2_s, rb2_r, ry_s, ry_r,
    cot2_s, cot2_r, c2_s, c2_r, p1_s, p1_r, p2_s, p2_r,
):
    mg = lax.axis_index("grp")
    mi = lax.axis_index("in")
    core = lax.rem(mi, 2)
    my_y = lax.div(mi, 2)
    sib = mi + 1 - 2 * core

    arriving, leaving = {}, []

    def rcopy(src, dst, ss, rs, dev):
        return pltpu.make_async_remote_copy(
            src_ref=src, dst_ref=dst, send_sem=ss, recv_sem=rs, device_id=dev, device_id_type=MESH
        )

    def each(n, body):
        def step(p, carry):
            body(p)
            return carry

        lax.fori_loop(1, n, step, 0)

    def arrives(name, ref, rs):
        arriving[name] = lambda: rcopy(ref, ref, rs, rs, (mg, sib)).wait_recv()

    def leaves(ref, ss):
        leaving.append(lambda: rcopy(ref, ref, ss, ss, (mg, sib)).wait_send())

    def wait(name):
        arriving.pop(name)()

    def grp_to(p):
        return lax.rem(mg + 7 * p, NG)

    def in_to(p):
        return lax.rem(mi + 3 * p, NI)

    def y_to(q):
        return lax.rem(mi + 2 * q, NI)

    def y_from(q):
        return lax.rem(mi + NI - 2 * q, NI)

    def to_grp(name, src, dst, ss, rs):
        def go(p):
            rcopy(src.at[grp_to(p)], dst.at[mg], ss, rs, (grp_to(p), mi)).start()

        each(NG, go)
        leaves(src.at[pl.ds(0, NG - 1)], ss)
        arrives(name, dst.at[pl.ds(0, NG - 1)], rs)

    def to_in(name, src, dst, ss, rs, left, came):
        def go(p):
            rcopy(src(in_to(p)), dst, ss, rs, (mg, in_to(p))).start()

        each(NI, go)
        leaves(left, ss)
        arrives(name, came, rs)

    my_z, my_x = lax.div(mg, 4), lax.rem(mg, 4)
    my_gz = lax.div(my_z, 2) * 4 + my_x

    def to_four(name, axis, src, dst, ss, rs, left, came):
        for q in range(1, 4):
            if axis == "x":
                n = lax.rem(my_x + q, 4)
                dev = (my_z * 4 + n, mi)
            elif axis == "z":
                n = lax.rem(my_z + q, 4)
                dev = (n * 4 + my_x, mi)
            else:
                n = lax.rem(my_y + q, 4)
                dev = (mg, n * 2 + core)
            rcopy(src(n), dst, ss, rs, dev).start()
        leaves(left, ss)
        arrives(name, came, rs)

    def to_sib(name, src, dst, ss, rs, came=None):
        rcopy(src, dst, ss, rs, (mg, sib)).start()
        leaves(src, ss)
        arrives(name, dst if came is None else came, rs)

    loads = [
        pltpu.make_async_copy(src, dst, load.at[n])
        for n, (src, dst) in enumerate(
            [(enc_hbm, enc_ref), (w_hbm, w_ref), (val_hbm, val_ref), (cot_hbm, cot_ref), (count_hbm, count_ref),
             (cols_hbm, cols_ref), (slot_hbm, slot_ref), (mask_hbm, mask_ref)]
        )
    ]
    for n in (6, 0, 1, 2, 4, 5, 7, 3):
        loads[n].start()

    seven = pl.ds(0, NI - 1)

    barrier = pltpu.get_barrier_semaphore()

    def greet(dev):
        pl.semaphore_signal(barrier, inc=1, device_id=dev, device_id_type=MESH)

    each(NG, lambda p: greet((grp_to(p), mi)))
    each(NI, lambda p: greet((mg, in_to(p))))

    def body():
        loads[6].wait()
        slot_row = slot_ref[...]
        eye = iota((ROWS, ROWS), 0) == iota((ROWS, ROWS), 1)
        slot_b = jnp.broadcast_to(slot_row, (ROWS, ROWS))
        slot_col = jnp.sum(jnp.where(eye, slot_b, 0), axis=1, keepdims=True)
        own_b = lax.shift_right_logical(slot_b, 7)
        own_col = lax.shift_right_logical(slot_col, 7)
        same = own_b == jnp.broadcast_to(own_col, (ROWS, ROWS))
        n_ix, m_ix = iota((ROWS, ROWS), 0), iota((ROWS, ROWS), 1)
        rank_row = jnp.sum(jnp.where(same & (n_ix < m_ix), 1, 0), axis=0, keepdims=True)
        rank_col = jnp.sum(jnp.where(same & (m_ix < n_ix), 1, 0), axis=1, keepdims=True)
        flat_row = lax.shift_right_logical(slot_row, 7) * 2 + rank_row
        flat_col = own_col * 2 + rank_col
        spread = iota((SLOTS, ROWS), 0) == jnp.broadcast_to(flat_row, (SLOTS, ROWS))
        spread_rows = ones_where(spread)
        place1 = jnp.bitwise_and(slot_col, ROWS - 1) + 1
        place_b = jnp.broadcast_to(place1, (ROWS, ROWS)).astype(F32).astype(BF)
        s_pl[...] = dot(spread_rows, place_b).astype(BF).reshape(NG, 16, ROWS)
        loads[0].wait()
        s_rows[...] = dot(spread_rows, enc_ref[...]).astype(BF).reshape(NG, 16, D)

        pl.semaphore_wait(barrier, (NG - 1) + (NI - 1))
        to_grp("pl", s_pl, r_pl, pl_s, pl_r)
        to_grp("rows", s_rows, r_rows, rows_s, rows_r)
        r_rows[mg] = s_rows[mg]

        r_pl[mg] = s_pl[mg]
        loads[1].wait()
        w_f32[...] = w_ref[...].astype(F32)
        to_sib("w0", w_f32, w_got, w0_s, w0_r)

        loads[2].wait()
        loads[4].wait()
        loads[5].wait()
        count = count_ref[0]
        for j in range(5):
            col = lax.rem(mi + j, NI)
            acc = jnp.zeros((ROWS, ROWS), F32)
            for k in range(10):
                live = jnp.logical_and(cols_ref[0, k] == col, count > k)
                acc = acc + val_ref[0, k].astype(F32) * jnp.where(live, 1.0, 0.0)
            adj_up[mi, j] = acc.astype(BF)
        wait("w0")
        first = core == 0
        pair = jnp.concatenate(
            [
                jnp.where(first, w_f32[...], w_got[...]),
                jnp.where(first, w_got[...], w_f32[...]),
            ],
            axis=0,
        )
        pair = jnp.where(first, pair[:, :512], pair[:, 512:]).astype(BF)
        mine_w = whole_w.at[core, my_z, my_x, my_y]
        mine_w[...] = pair
        to_four(
            "w1", "y", lambda n: mine_w, mine_w, w1_s, w1_r,
            whole_w.at[core, 0, 0, pl.ds(0, 3)], whole_w.at[core, 0, 0, pl.ds(0, 3)],
        )

        mine_up = adj_up.at[mi]
        for q in (1, 3):
            rcopy(mine_up, mine_up, a_s.at[q], a_r.at[q], (mg, y_to(q))).start()
            leaves(mine_up, a_s.at[q])
            arrives("a%d" % q, mine_up, a_r.at[q])
        to_sib("a0", mine_up, mine_up, a_s.at[0], a_r.at[0])


        loads[7].wait()
        labelled = mask_ref[...] > 0
        spread_cot = ones_where(spread & jnp.broadcast_to(labelled, (SLOTS, ROWS)))

        def even_first(g):
            return (
                jnp.bitwise_and(g, 4) * 2
                + lax.shift_right_logical(jnp.bitwise_and(g, 8), 1)
                + jnp.bitwise_and(g, 3)
            )

        own_row = lax.shift_right_logical(slot_row, 7)
        flat_in = (
            jnp.bitwise_and(own_row, 7) * 32
            + even_first(lax.shift_right_logical(own_row, 3)) * 2 + rank_row
        )
        spread_in = ones_where(
            iota((SLOTS, ROWS), 0)
            == jnp.broadcast_to(jnp.where(labelled, flat_in, -1), (SLOTS, ROWS))
        )
        loads[3].wait()
        s_cot2[...] = dot(spread_in, cot_ref[:, 512:]).astype(BF).reshape(NI, 32, 512)
        to_in(
            "cot2", lambda i: s_cot2.at[i], r_cot2.at[mi], cot2_s, cot2_r,
            s_cot2.at[seven], r_cot2.at[seven],
        )
        r_cot2[mi] = s_cot2[mi]
        s_cot[...] = dot(spread_cot, cot_ref[:, :512]).astype(BF).reshape(NG, 16, 512)
        to_grp("cot", s_cot, r_cot, cot_s, cot_r)
        r_cot[mg] = s_cot[mg]

        collect = ones_where(
            iota((ROWS, SLOTS), 1) == jnp.broadcast_to(flat_col, (ROWS, SLOTS))
        )
        flat_out = (
            jnp.bitwise_and(own_col, 7) * 32
            + even_first(lax.shift_right_logical(own_col, 3)) * 2 + rank_col
        )
        collect_out = ones_where(
            iota((ROWS, SLOTS), 1) == jnp.broadcast_to(flat_out, (ROWS, SLOTS))
        )

        r_ix, c_ix = iota((SLOTS, SLOTS), 0), iota((SLOTS, SLOTS), 1)

        def moved(ix):
            z = jnp.bitwise_and(lax.shift_right_logical(ix, 2), 2) + jnp.bitwise_and(
                lax.shift_right_logical(ix, 4), 1
            )
            x = jnp.bitwise_and(lax.shift_right_logical(ix, 1), 3)
            return (
                (z * 4 + x) * 16 + lax.shift_right_logical(ix, 5) * 2 + jnp.bitwise_and(ix, 1)
            )

        perm = ones_where(c_ix == moved(r_ix))
        perm_t = ones_where(r_ix == moved(c_ix))
        low = (jnp.bitwise_and(r_ix, 31) == jnp.bitwise_and(c_ix, 31)) & (
            lax.shift_right_logical(c_ix, 5) == mi
        )
        o_rows = ones_where(
            iota((16, SLOTS), 0) == lax.shift_right_logical(iota((16, SLOTS), 1), 5)
        )

        wait("pl")
        pl_cols = dot(perm, r_pl[...].reshape(SLOTS, ROWS))
        pl_wide = jnp.concatenate([pl_cols, pl_cols], axis=1)
        v_all[mi] = dot(o_rows, jnp.where(low, pl_wide, 0.0).astype(BF)).astype(BF)
        to_in("v", lambda i: v_all.at[mi], v_all.at[mi], v_s, v_r, v_all.at[seven], v_all.at[seven])

        three, left_w, right_w = pl.ds(0, 3), pl.ds(0, 256), pl.ds(256, 256)
        wait("w1")
        group_l = whole_w.at[core, my_z, my_x, :, :, left_w]
        group_r = whole_w.at[core, my_z, my_x, :, :, right_w]
        some = whole_w.at[core, 0, three, :, :, left_w]
        to_four("w2l", "x", lambda n: group_l, group_l, w2_s.at[0], w2_r.at[0], some, some)
        to_four("w2r", "z", lambda n: group_r, group_r, w2_s.at[1], w2_r.at[1], some, some)

        for q, h in ((1, 2), (3, 4)):
            wait("a%d" % q)
            ref = adj_up.at[y_from(q), :, pl.ds(0 if q == 1 else 64, 64)]
            rcopy(ref, ref, a_s.at[h], a_r.at[h], (mg, y_to(q))).start()
            leaves(ref, a_s.at[h])
            arrives("a%d" % h, ref, a_r.at[h])
        wait("rows")
        for f in range(NI):
            part = r_rows[:, :, f * 128:(f + 1) * 128].reshape(SLOTS, 128)
            q_rows[f] = dot(perm, part).astype(BF).reshape(NI, 32, 128)
        to_in(
            "x", lambda i: q_rows.at[i], x_slots.at[:, mi], x_s, x_r,
            q_rows.at[seven], x_slots.at[:, seven],
        )
        x_slots[:, mi] = q_rows[mi]

        wait("a2")
        wait("a4")
        for q in range(1, 4):
            ref = adj_up.at[y_from(q)]
            to_sib(
                "f%d" % q, ref, ref, f_s.at[q], f_r.at[q],
                adj_up.at[lax.rem(sib + NI - 2 * q, NI)],
            )
        wait("cot")
        q_cot[...] = dot(perm, r_cot[...].reshape(SLOTS, 512)).astype(BF).reshape(NI, 32, 512)
        to_in(
            "c", lambda i: q_cot.at[i], c_slots.at[mi], c_s, c_r, q_cot.at[seven], c_slots.at[seven]
        )
        c_slots[mi] = q_cot[mi]

        wait("w2l")
        wait("w2r")
        plane_l = whole_w.at[core, my_z, :, :, :, left_w]
        plane_r = whole_w.at[core, :, my_x, :, :, right_w]
        some = whole_w.at[core, three, :, :, :, left_w]
        to_four("w3l", "z", lambda n: plane_l, plane_l, w2_s.at[2], w2_r.at[2], some, some)
        to_four("w3r", "x", lambda n: plane_r, plane_r, w2_s.at[3], w2_r.at[3], some, some)


        wait("cot2")
        q_cot2[...] = dot(perm_t, r_cot2[...].reshape(SLOTS, 512)).astype(BF).reshape(NG, 16, 512)
        to_grp("c2", q_cot2, c_slots2, c2_s, c2_r)
        c_slots2[mg] = q_cot2[mg]

        wait("v")
        v_sum = v_all[0].astype(F32)
        for i in range(1, NI):
            v_sum = v_sum + v_all[i].astype(F32)
        node1 = (iota((ROWS, SLOTS), 0) + 1).astype(F32)
        for o in range(NI):
            here = jnp.where(node1 == jnp.broadcast_to(v_sum[o:o + 1, :], (ROWS, SLOTS)), 1.0, 0.0)
            place[o] = here.astype(BF)
            place_t[o] = here.T.astype(BF)

        for name in ("a0", "f1", "f2", "f3"):
            wait(name)
        for r in range(NI):
            for j in range(5):
                c = (r + j) % NI
                adj[r * 128:(r + 1) * 128, c * 128:(c + 1) * 128] = adj_up[r, j]
                if 0 < j < 4:
                    flipped = adj_up[r, j].astype(F32).T.astype(BF)
                    adj[c * 128:(c + 1) * 128, r * 128:(r + 1) * 128] = flipped

        wait("x")
        feats = jnp.concatenate(
            [dot(place[o], x_slots[o].reshape(SLOTS, 128)).astype(BF) for o in range(NI)], axis=0
        )
        mixed[...] = dot(adj[...], feats).astype(BF).reshape(NI, ROWS, 128)
        my_rows = mixed_pair.at[0]
        my_cols = pl.ds(pl.multiple_of(mi * 128, 128), 128)
        to_in(
            "m", lambda i: mixed.at[i], my_rows.at[:, my_cols], m_s, m_r,
            mixed.at[seven], my_rows.at[:, pl.ds(0, 7 * 128)],
        )
        my_rows[:, my_cols] = mixed[mi]

        wait("w3l")
        wait("w3r")
        to_sib("w3", whole_w.at[core], whole_w.at[core], w3_s, w3_r, whole_w.at[1 - core])

        wait("c")
        place_out = dot(place[mi], perm).astype(BF)
        wait("c2")
        own_cot = (
            dot(place[mi], c_slots[...].reshape(SLOTS, 512)),
            dot(place_out, c_slots2[...].reshape(SLOTS, 512)),
        )

        wait("w3")
        wait("m")
        to_sib("ms", my_rows, mixed_pair.at[1], ms_s, ms_r)
        rows_val = mixed_pair[0]
        for h in range(2):
            v = dot(rows_val, whole_w[h].reshape(D, 512))
            k0 = 0.7978845608028654
            th = jnp.tanh(k0 * (v + 0.044715 * (v * v * v)))
            act = 0.5 * v * (1.0 + th)
            slope = 0.5 * (1.0 + th) + 0.5 * v * (1.0 - th * th) * (k0 * (1.0 + 3 * 0.044715 * (v * v)))
            g_half[h] = (own_cot[h] * slope).astype(BF)
            out_ref[:, h * 512:(h + 1) * 512] = act.astype(BF)

        to_sib("g", g_half.at[1 - core], g_pair.at[1], g_s, g_r)
        g_pair[0] = g_half[core]

        for f in range(NI):
            w_rows = whole_w[:, f // 2, f % 2 * 2:f % 2 * 2 + 2]
            gf_out[f] = (
                dot_t1(g_half[0], w_rows[0].reshape(128, 512))
                + dot_t1(g_half[1], w_rows[1].reshape(128, 512))
            ).astype(BF)
        to_in("gf", lambda i: gf_out.at[i], gf_in.at[mi], gf_s, gf_r, gf_out.at[seven], gf_in.at[seven])
        gf_in[mi] = gf_out[mi]

        o_slots[...] = dot_t0(place_out, out_ref[:, :512]).astype(BF).reshape(NG, 16, 512)
        to_grp("o1", o_slots, o_mid, o1_s, o1_r)
        o_mid[mg] = o_slots[mg]
        p_slots[...] = dot_t0(place[mi], out_ref[:, 512:]).astype(BF).reshape(NI, 32, 512)
        to_in("p1", lambda i: p_slots.at[i], p_mid.at[mi], p1_s, p1_r, p_slots.at[seven], p_mid.at[seven])
        p_mid[mi] = p_slots[mi]

        wait("ms")
        wait("g")
        m_val = mixed_pair[...].reshape(2 * ROWS, D)
        for h in range(2):
            term = dot_t0(m_val, g_pair[:, :, h * 256:(h + 1) * 256].reshape(2 * ROWS, 256))
            term = term.astype(BF).reshape(4, 4, 64, 256)
            for n in range(4):
                if h == 0:
                    wa[n] = term[:, n]
                else:
                    wb[n] = term[n]
        to_four("ra", "x", lambda n: wa.at[n], wa_in.at[my_x], ra_s, ra_r, wa.at[three], wa.at[three])
        to_four("rb", "z", lambda n: wb.at[n], wb_in.at[my_z], rb_s, rb_r, wb.at[three], wb.at[three])
        wa_in[my_x] = wa[my_x]
        wb_in[my_z] = wb[my_z]

        wait("gf")
        feed = gf_in[...].reshape(D, 128)
        back = dot(adj[...], feed).astype(BF)
        for o in range(NI):
            z_slots[:, o] = (
                dot(place_t[o], back[o * 128:(o + 1) * 128]).astype(BF).reshape(NI, 32, 128)
            )
        for h in range(2):
            rows_h = pl.ds(h * 16, 16)
            to_in(
                "z1%d" % h, lambda i: z_slots.at[i, :, rows_h], z_mid.at[mi, :, rows_h],
                z1_s.at[h], z1_r.at[h], z_slots.at[seven, :, rows_h], z_mid.at[seven, :, rows_h],
            )
        z_mid[mi] = z_slots[mi]


        def add(ref):
            out = ref[0].astype(F32)
            for n in range(1, 4):
                out = out + ref[n].astype(F32)
            return out

        wait("p1")
        p_send[...] = dot(perm_t, p_mid[...].reshape(SLOTS, 512)).astype(BF).reshape(NG, 16, 512)
        to_grp("p2", p_send, p_back, p2_s, p2_r)
        p_back[mg] = p_send[mg]

        wait("o1")
        o_send[...] = dot(perm, o_mid[...].reshape(SLOTS, 512)).astype(BF).reshape(NI, 32, 512)
        to_in("o2", lambda i: o_send.at[i], o_back.at[mi], o2_s, o2_r, o_send.at[seven], o_back.at[seven])
        o_back[mi] = o_send[mi]

        wait("ra")
        wa_sum[...] = add(wa_in).astype(BF)
        wait("rb")
        wb_sum[...] = add(wb_in).astype(BF)
        part = wa_sum.at[three]
        to_four("ra2", "z", lambda n: wa_sum.at[n], wa_in2.at[my_z], ra2_s, ra2_r, part, part)
        to_four("rb2", "x", lambda n: wb_sum.at[n], wb_in2.at[my_x], rb2_s, rb2_r, part, part)
        wa_in2[my_z] = wa_sum[my_z]
        wb_in2[my_x] = wb_sum[my_x]

        pz_r, pz_c = iota((ROWS, ROWS), 0), iota((ROWS, ROWS), 1)
        perm_z = ones_where(
            pz_c == jnp.bitwise_and(lax.shift_right_logical(pz_r, 1), 7) * 16
            + lax.shift_right_logical(pz_r, 4) * 2 + jnp.bitwise_and(pz_r, 1)
        )
        for h in range(2):
            wait("z1%d" % h)
            for f in range(NI):
                z_send[h * 8:(h + 1) * 8, :, f * 128:(f + 1) * 128] = (
                    dot(perm_z, z_mid[f, :, h * 16:(h + 1) * 16].reshape(ROWS, 128))
                    .astype(BF).reshape(8, 16, 128)
                )

            def go(p, carry):
                n = jnp.bitwise_and(my_gz + p, 7)
                dest = lax.div(n, 4) * 8 + h * 4 + lax.rem(n, 4)

                @pl.when(dest != mg)
                def _():
                    rcopy(z_send.at[h * 8 + n], z_back.at[mg], z2_s, z2_r, (dest, mi)).start()

                return carry

            lax.fori_loop(0, 8, go, 0)
        leaves(z_send.at[pl.ds(0, NG - 1)], z2_s)
        arrives("z2", z_back.at[pl.ds(0, NG - 1)], z2_r)
        z_back[mg] = z_send[lax.rem(my_z, 2) * 8 + my_gz]

        wait("ra2")
        wait("rb2")
        wy[:, :, :256] = add(wa_in2).reshape(NI, 8, 256)
        wy[:, :, 256:] = add(wb_in2).reshape(NI, 8, 256)
        to_in("ry", lambda i: wy.at[i], wy_in.at[mi], ry_s, ry_r, wy.at[seven], wy_in.at[seven])
        wy_in[mi] = wy[mi]
        wait("o2")
        out_ref[:, :512] = dot(collect_out, o_back[...].reshape(SLOTS, 512)).astype(BF)
        wait("p2")
        out_ref[:, 512:] = dot(collect, p_back[...].reshape(SLOTS, 512)).astype(BF)
        wait("ry")
        for c in range(2):
            half = wy_in[c]
            for n in range(1, 4):
                half = half + wy_in[2 * n + c]
            wgrad_ref[:, c * 512:(c + 1) * 512] = half * (1.0 / 128)
        wait("z2")
        grad_ref[...] = dot(collect, z_back[...].reshape(SLOTS, D)).astype(BF)

    body()
    for name in list(arriving):
        wait(name)
    for done in leaving:
        done()


def hand_over(a, b, c, a_out, b_out, c_out, sem):
    copies = [
        pltpu.make_async_copy(src, dst, sem.at[n])
        for n, (src, dst) in enumerate([(a, a_out), (b, b_out), (c, c_out)])
    ]
    for copy in copies:
        copy.start()
    for copy in copies:
        copy.wait()


def scratch():
    v = pltpu.VMEM
    dma = pltpu.SemaphoreType.DMA
    big, small = v((4, 4, 64, 256), BF), v((4, 64, 256), BF)
    grp_rows = v((NG, 16, D), BF)
    grp_half, in_half = v((NG, 16, 512), BF), v((NI, 32, 512), BF)
    bufs = [
        pltpu.SMEM((1, 10), I32),
        v((1, ROWS), I32), v((1, ROWS), I32), pltpu.SMEM((1,), I32), v((ROWS, D), BF), v((ROWS, D), BF), v((8, D), BF), v((1, 10, ROWS, ROWS), BF),
        grp_rows, grp_rows, v((NG, 16, ROWS), BF), v((NG, 16, ROWS), BF),
        grp_half, grp_half, in_half, in_half,
        v((8, D), F32), v((8, D), F32), v((2, 4, 4, 4, 16, 512), BF), v((NI, 5, ROWS, ROWS), BF),
        v((D, D), BF),
        v((NI, NI, 32, 128), BF), v((NI, NI, 32, 128), BF), v((NI, 16, SLOTS), BF),
        in_half, in_half, grp_half, grp_half, v((NI, ROWS, SLOTS), BF), v((NI, SLOTS, ROWS), BF),
        v((NI, ROWS, 128), BF), v((2, ROWS, D), BF),
        v((2, ROWS, 512), BF), v((2, ROWS, 512), BF), v((NI, ROWS, 128), BF), v((NI, ROWS, 128), BF),
        grp_half, grp_half, in_half, in_half, in_half, in_half, grp_half, grp_half,
        v((NI, NI, 32, 128), BF), v((NI, NI, 32, 128), BF), grp_rows, grp_rows,
        big, big, big, big, small, small, small, small, v((NI, 8, 512), F32), v((NI, 8, 512), F32),
    ]
    one, two, four, five = dma, dma((2,)), dma((4,)), dma((5,))
    sems = [dma((8,))]
    for s in [one] * 5 + [four] + [one] + [five, four] + [one] * 9 + [two] + [one] * 10:
        sems += [s, s]
    return bufs + sems


def per_device(
    encoded, owner_slot, label_mask, cotangent, weight, block_cols, block_counts, block_values
):
    anywhere = pl.BlockSpec(memory_space=pl.ANY)
    vm = pl.BlockSpec(memory_space=pltpu.VMEM)
    results = pl.pallas_call(
        kernel,
        out_shape=(
            pltpu.VMEM((ROWS, D), BF), pltpu.VMEM((ROWS, D), BF), pltpu.VMEM((8, D), F32),
        ),
        in_specs=[anywhere] * 8,
        out_specs=(vm,) * 3,
        scratch_shapes=scratch(),
        compiler_params=pltpu.CompilerParams(
            collective_id=0, has_side_effects=True, vmem_limit_bytes=58 * 1024 * 1024
        ),
    )(
        block_cols, owner_slot.reshape(1, ROWS), label_mask.reshape(1, ROWS),
        block_counts, encoded, cotangent, weight, block_values,
    )
    return tuple(pl.pallas_call(
        hand_over,
        out_shape=tuple(jax.ShapeDtypeStruct(r.shape, r.dtype) for r in results),
        in_specs=[vm] * 3,
        out_specs=(anywhere,) * 3,
        scratch_shapes=[pltpu.SemaphoreType.DMA((3,))],
    )(*[pltpu.with_memory_space_constraint(r, pltpu.VMEM) for r in results]))


def solution(mesh):
    rows = P(("grp", "in"), None)
    flat = P(("grp", "in"))
    in_specs = (rows, flat, flat, rows, rows, rows, flat, P(("grp", "in"), None, None, None))
    return jax.shard_map(
        per_device, mesh=mesh, in_specs=in_specs, out_specs=(rows, rows, rows), check_vma=False
    )
```

```python
import functools

import jax
import jax.numpy as jnp
from jax import lax
from jax.experimental import pallas as pl
from jax.experimental.pallas import tpu as pltpu
from jax.sharding import PartitionSpec as P

MESH = pl.DeviceIdType.MESH
BF = jnp.bfloat16
F32 = jnp.float32
I32 = jnp.int32

NG = 16
NI = 8
ROWS = 128
D = 1024
SLOTS = 256


def iota(shape, dim):
    return lax.broadcasted_iota(I32, shape, dim)


def ones_where(cond):
    return jnp.where(cond, 1.0, 0.0).astype(BF)


def dot(a, b):
    return jnp.dot(a, b, preferred_element_type=F32)


def dot_t0(a, b):
    return lax.dot_general(a, b, (((0,), (0,)), ((), ())), preferred_element_type=F32)


def dot_t1(a, b):
    return lax.dot_general(a, b, (((1,), (1,)), ((), ())), preferred_element_type=F32)


def kernel(
    cols_hbm, slot_hbm, mask_hbm, count_hbm, enc_hbm, cot_hbm, w_hbm, val_hbm,
    out_ref, grad_ref, wgrad_ref,
    cols_ref, slot_ref, mask_ref, count_ref, enc_ref, cot_ref, w_ref, val_ref,
    s_rows, r_rows, s_pl, r_pl, s_cot, r_cot, s_cot2, r_cot2,
    w_f32, w_got, whole_w, adj_up, adj,
    q_rows, x_slots, v_all, q_cot, c_slots, q_cot2, c_slots2, place, place_t,
    mixed, mixed_pair,
    g_half, g_pair, gf_out, gf_in,
    o_slots, o_mid, o_send, o_back,
    p_slots, p_mid, p_send, p_back,
    z_slots, z_mid, z_send, z_back,
    wa, wb, wa_in, wb_in, wa_sum, wb_sum, wa_in2, wb_in2, wy, wy_in,
    load,
    rows_s, rows_r, pl_s, pl_r, cot_s, cot_r,
    w0_s, w0_r, w1_s, w1_r, w2_s, w2_r, w3_s, w3_r,
    a_s, a_r, f_s, f_r,
    x_s, x_r, v_s, v_r, c_s, c_r,
    m_s, m_r, ms_s, ms_r,
    g_s, g_r, gf_s, gf_r,
    o1_s, o1_r, o2_s, o2_r,
    z1_s, z1_r, z2_s, z2_r,
    ra_s, ra_r, rb_s, rb_r, ra2_s, ra2_r, rb2_s, rb2_r, ry_s, ry_r,
    cot2_s, cot2_r, c2_s, c2_r, p1_s, p1_r, p2_s, p2_r,
):
    mg = lax.axis_index("grp")
    mi = lax.axis_index("in")
    core = lax.rem(mi, 2)
    my_y = lax.div(mi, 2)
    sib = mi + 1 - 2 * core

    arriving, leaving = {}, []

    def rcopy(src, dst, ss, rs, dev):
        return pltpu.make_async_remote_copy(
            src_ref=src, dst_ref=dst, send_sem=ss, recv_sem=rs, device_id=dev, device_id_type=MESH
        )

    def each(n, body):
        def step(p, carry):
            body(p)
            return carry

        lax.fori_loop(1, n, step, 0)

    def arrives(name, ref, rs):
        arriving[name] = lambda: rcopy(ref, ref, rs, rs, (mg, sib)).wait_recv()

    def leaves(ref, ss):
        leaving.append(lambda: rcopy(ref, ref, ss, ss, (mg, sib)).wait_send())

    def wait(name):
        arriving.pop(name)()

    def grp_to(p):
        return lax.rem(mg + 7 * p, NG)

    def in_to(p):
        return lax.rem(mi + 3 * p, NI)

    def y_to(q):
        return lax.rem(mi + 2 * q, NI)

    def y_from(q):
        return lax.rem(mi + NI - 2 * q, NI)

    def to_grp(name, src, dst, ss, rs):
        def go(p):
            rcopy(src.at[grp_to(p)], dst.at[mg], ss, rs, (grp_to(p), mi)).start()

        each(NG, go)
        leaves(src.at[pl.ds(0, NG - 1)], ss)
        arrives(name, dst.at[pl.ds(0, NG - 1)], rs)

    def to_in(name, src, dst, ss, rs, left, came):
        def go(p):
            rcopy(src(in_to(p)), dst, ss, rs, (mg, in_to(p))).start()

        each(NI, go)
        leaves(left, ss)
        arrives(name, came, rs)

    my_z, my_x = lax.div(mg, 4), lax.rem(mg, 4)
    my_gz = lax.div(my_z, 2) * 4 + my_x

    def to_four(name, axis, src, dst, ss, rs, left, came):
        for q in range(1, 4):
            if axis == "x":
                n = lax.rem(my_x + q, 4)
                dev = (my_z * 4 + n, mi)
            elif axis == "z":
                n = lax.rem(my_z + q, 4)
                dev = (n * 4 + my_x, mi)
            else:
                n = lax.rem(my_y + q, 4)
                dev = (mg, n * 2 + core)
            rcopy(src(n), dst, ss, rs, dev).start()
        leaves(left, ss)
        arrives(name, came, rs)

    def to_sib(name, src, dst, ss, rs, came=None):
        rcopy(src, dst, ss, rs, (mg, sib)).start()
        leaves(src, ss)
        arrives(name, dst if came is None else came, rs)

    loads = [
        pltpu.make_async_copy(src, dst, load.at[n])
        for n, (src, dst) in enumerate(
            [(enc_hbm, enc_ref), (w_hbm, w_ref), (val_hbm, val_ref), (cot_hbm, cot_ref), (count_hbm, count_ref),
             (cols_hbm, cols_ref), (slot_hbm, slot_ref), (mask_hbm, mask_ref)]
        )
    ]
    for n in (6, 0, 1, 2, 4, 5, 7, 3):
        loads[n].start()

    seven = pl.ds(0, NI - 1)

    def side(h):
        return lax.rem(my_z + h, 2)

    barrier = pltpu.get_barrier_semaphore()

    def greet(dev):
        pl.semaphore_signal(barrier, inc=1, device_id=dev, device_id_type=MESH)

    each(NG, lambda p: greet((grp_to(p), mi)))
    each(NI, lambda p: greet((mg, in_to(p))))

    def body():
        loads[6].wait()
        slot_row = slot_ref[...]
        eye = iota((ROWS, ROWS), 0) == iota((ROWS, ROWS), 1)
        slot_b = jnp.broadcast_to(slot_row, (ROWS, ROWS))
        slot_col = jnp.sum(jnp.where(eye, slot_b, 0), axis=1, keepdims=True)
        own_b = lax.shift_right_logical(slot_b, 7)
        own_col = lax.shift_right_logical(slot_col, 7)
        same = own_b == jnp.broadcast_to(own_col, (ROWS, ROWS))
        n_ix, m_ix = iota((ROWS, ROWS), 0), iota((ROWS, ROWS), 1)
        rank_row = jnp.sum(jnp.where(same & (n_ix < m_ix), 1, 0), axis=0, keepdims=True)
        rank_col = jnp.sum(jnp.where(same & (m_ix < n_ix), 1, 0), axis=1, keepdims=True)
        flat_row = lax.shift_right_logical(slot_row, 7) * 2 + rank_row
        flat_col = own_col * 2 + rank_col
        spread = iota((SLOTS, ROWS), 0) == jnp.broadcast_to(flat_row, (SLOTS, ROWS))
        spread_rows = ones_where(spread)
        place1 = jnp.bitwise_and(slot_col, ROWS - 1) + 1
        place_b = jnp.broadcast_to(place1, (ROWS, ROWS)).astype(F32).astype(BF)
        s_pl[...] = dot(spread_rows, place_b).astype(BF).reshape(NG, 16, ROWS)
        loads[0].wait()
        s_rows[...] = dot(spread_rows, enc_ref[...]).astype(BF).reshape(NG, 16, D)

        pl.semaphore_wait(barrier, (NG - 1) + (NI - 1))
        to_grp("pl", s_pl, r_pl, pl_s, pl_r)
        to_grp("rows", s_rows, r_rows, rows_s, rows_r)
        r_rows[mg] = s_rows[mg]

        r_pl[mg] = s_pl[mg]
        loads[1].wait()
        w_f32[...] = w_ref[...].astype(F32)
        to_sib("w0", w_f32, w_got, w0_s, w0_r)

        loads[2].wait()
        loads[4].wait()
        loads[5].wait()
        count = count_ref[0]
        for j in range(5):
            col = lax.rem(mi + j, NI)
            acc = jnp.zeros((ROWS, ROWS), F32)
            for k in range(10):
                live = jnp.logical_and(cols_ref[0, k] == col, count > k)
                acc = acc + val_ref[0, k].astype(F32) * jnp.where(live, 1.0, 0.0)
            adj_up[mi, j] = acc.astype(BF)
        wait("w0")
        first = core == 0
        pair = jnp.concatenate(
            [
                jnp.where(first, w_f32[...], w_got[...]),
                jnp.where(first, w_got[...], w_f32[...]),
            ],
            axis=0,
        )
        pair = jnp.where(first, pair[:, :512], pair[:, 512:]).astype(BF)
        mine_w = whole_w.at[core, my_z, my_x, my_y]
        mine_w[...] = pair
        to_four(
            "w1", "y", lambda n: mine_w, mine_w, w1_s, w1_r,
            whole_w.at[core, 0, 0, pl.ds(0, 3)], whole_w.at[core, 0, 0, pl.ds(0, 3)],
        )

        mine_up = adj_up.at[mi]
        for q in (1, 3):
            rcopy(mine_up, mine_up, a_s.at[q], a_r.at[q], (mg, y_to(q))).start()
            leaves(mine_up, a_s.at[q])
            arrives("a%d" % q, mine_up, a_r.at[q])
        to_sib("a0", mine_up, mine_up, a_s.at[0], a_r.at[0])


        loads[7].wait()
        labelled = mask_ref[...] > 0
        spread_cot = ones_where(spread & jnp.broadcast_to(labelled, (SLOTS, ROWS)))

        def even_first(g):
            return (
                jnp.bitwise_and(g, 4) * 2
                + lax.shift_right_logical(jnp.bitwise_and(g, 8), 1)
                + jnp.bitwise_and(g, 3)
            )

        own_row = lax.shift_right_logical(slot_row, 7)
        flat_in = (
            jnp.bitwise_and(own_row, 7) * 32
            + even_first(lax.shift_right_logical(own_row, 3)) * 2 + rank_row
        )
        spread_in = ones_where(
            iota((SLOTS, ROWS), 0)
            == jnp.broadcast_to(jnp.where(labelled, flat_in, -1), (SLOTS, ROWS))
        )
        loads[3].wait()
        s_cot2[...] = dot(spread_in, cot_ref[:, 512:]).astype(BF).reshape(NI, 32, 512)
        to_in(
            "cot2", lambda i: s_cot2.at[i], r_cot2.at[mi], cot2_s, cot2_r,
            s_cot2.at[seven], r_cot2.at[seven],
        )
        r_cot2[mi] = s_cot2[mi]
        s_cot[...] = dot(spread_cot, cot_ref[:, :512]).astype(BF).reshape(NG, 16, 512)
        to_grp("cot", s_cot, r_cot, cot_s, cot_r)
        r_cot[mg] = s_cot[mg]

        collect = ones_where(
            iota((ROWS, SLOTS), 1) == jnp.broadcast_to(flat_col, (ROWS, SLOTS))
        )
        flat_out = (
            jnp.bitwise_and(own_col, 7) * 32
            + even_first(lax.shift_right_logical(own_col, 3)) * 2 + rank_col
        )
        collect_out = ones_where(
            iota((ROWS, SLOTS), 1) == jnp.broadcast_to(flat_out, (ROWS, SLOTS))
        )

        r_ix, c_ix = iota((SLOTS, SLOTS), 0), iota((SLOTS, SLOTS), 1)

        def moved(ix):
            z = jnp.bitwise_and(lax.shift_right_logical(ix, 2), 2) + jnp.bitwise_and(
                lax.shift_right_logical(ix, 4), 1
            )
            x = jnp.bitwise_and(lax.shift_right_logical(ix, 1), 3)
            return (
                (z * 4 + x) * 16 + lax.shift_right_logical(ix, 5) * 2 + jnp.bitwise_and(ix, 1)
            )

        perm = ones_where(c_ix == moved(r_ix))
        perm_t = ones_where(r_ix == moved(c_ix))
        low = (jnp.bitwise_and(r_ix, 31) == jnp.bitwise_and(c_ix, 31)) & (
            lax.shift_right_logical(c_ix, 5) == mi
        )
        o_rows = ones_where(
            iota((16, SLOTS), 0) == lax.shift_right_logical(iota((16, SLOTS), 1), 5)
        )

        wait("pl")
        pl_cols = dot(perm, r_pl[...].reshape(SLOTS, ROWS))
        pl_wide = jnp.concatenate([pl_cols, pl_cols], axis=1)
        v_all[mi] = dot(o_rows, jnp.where(low, pl_wide, 0.0).astype(BF)).astype(BF)
        to_in("v", lambda i: v_all.at[mi], v_all.at[mi], v_s, v_r, v_all.at[seven], v_all.at[seven])

        three, left_w, right_w = pl.ds(0, 3), pl.ds(0, 256), pl.ds(256, 256)
        wait("w1")
        group_l = whole_w.at[core, my_z, my_x, :, :, left_w]
        group_r = whole_w.at[core, my_z, my_x, :, :, right_w]
        some = whole_w.at[core, 0, three, :, :, left_w]
        to_four("w2l", "x", lambda n: group_l, group_l, w2_s.at[0], w2_r.at[0], some, some)
        to_four("w2r", "z", lambda n: group_r, group_r, w2_s.at[1], w2_r.at[1], some, some)

        for q, h in ((1, 2), (3, 4)):
            wait("a%d" % q)
            ref = adj_up.at[y_from(q), :, pl.ds(0 if q == 1 else 64, 64)]
            rcopy(ref, ref, a_s.at[h], a_r.at[h], (mg, y_to(q))).start()
            leaves(ref, a_s.at[h])
            arrives("a%d" % h, ref, a_r.at[h])
        wait("rows")
        for f in range(NI):
            part = r_rows[:, :, f * 128:(f + 1) * 128].reshape(SLOTS, 128)
            q_rows[f] = dot(perm, part).astype(BF).reshape(NI, 32, 128)
        to_in(
            "x", lambda i: q_rows.at[i], x_slots.at[:, mi], x_s, x_r,
            q_rows.at[seven], x_slots.at[:, seven],
        )
        x_slots[:, mi] = q_rows[mi]

        wait("w2l")
        wait("w2r")
        plane_l = whole_w.at[core, my_z, :, :, :, left_w]
        plane_r = whole_w.at[core, :, my_x, :, :, right_w]
        some = whole_w.at[core, three, :, :, :, left_w]
        to_four("w3l", "z", lambda n: plane_l, plane_l, w2_s.at[2], w2_r.at[2], some, some)
        to_four("w3r", "x", lambda n: plane_r, plane_r, w2_s.at[3], w2_r.at[3], some, some)


        wait("cot2")
        q_cot2[...] = dot(perm_t, r_cot2[...].reshape(SLOTS, 512)).astype(BF).reshape(NG, 16, 512)
        to_grp("c2", q_cot2, c_slots2, c2_s, c2_r)
        c_slots2[mg] = q_cot2[mg]

        wait("a2")
        wait("a4")
        for q in range(1, 4):
            ref = adj_up.at[y_from(q)]
            to_sib(
                "f%d" % q, ref, ref, f_s.at[q], f_r.at[q],
                adj_up.at[lax.rem(sib + NI - 2 * q, NI)],
            )

        wait("v")
        v_sum = v_all[0].astype(F32)
        for i in range(1, NI):
            v_sum = v_sum + v_all[i].astype(F32)
        node1 = (iota((ROWS, SLOTS), 0) + 1).astype(F32)
        for o in range(NI):
            here = jnp.where(node1 == jnp.broadcast_to(v_sum[o:o + 1, :], (ROWS, SLOTS)), 1.0, 0.0)
            place[o] = here.astype(BF)
            place_t[o] = here.T.astype(BF)

        for name in ("a0", "f1", "f2", "f3"):
            wait(name)
        for r in range(NI):
            for j in range(5):
                c = (r + j) % NI
                adj[r * 128:(r + 1) * 128, c * 128:(c + 1) * 128] = adj_up[r, j]
                if 0 < j < 4:
                    flipped = adj_up[r, j].astype(F32).T.astype(BF)
                    adj[c * 128:(c + 1) * 128, r * 128:(r + 1) * 128] = flipped

        wait("cot")
        q_cot[...] = dot(perm, r_cot[...].reshape(SLOTS, 512)).astype(BF).reshape(NI, 32, 512)
        to_in(
            "c", lambda i: q_cot.at[i], c_slots.at[mi], c_s, c_r, q_cot.at[seven], c_slots.at[seven]
        )
        c_slots[mi] = q_cot[mi]

        wait("x")
        feats = jnp.concatenate(
            [dot(place[o], x_slots[o].reshape(SLOTS, 128)).astype(BF) for o in range(NI)], axis=0
        )
        mixed[...] = dot(adj[...], feats).astype(BF).reshape(NI, ROWS, 128)
        my_rows = mixed_pair.at[0]
        my_cols = pl.ds(pl.multiple_of(mi * 128, 128), 128)
        to_in(
            "m", lambda i: mixed.at[i], my_rows.at[:, my_cols], m_s, m_r,
            mixed.at[seven], my_rows.at[:, pl.ds(0, 7 * 128)],
        )
        my_rows[:, my_cols] = mixed[mi]

        wait("w3l")
        wait("w3r")
        to_sib("w3", whole_w.at[core], whole_w.at[core], w3_s, w3_r, whole_w.at[1 - core])

        wait("c")
        place_out = dot(place[mi], perm).astype(BF)
        wait("c2")
        own_cot = (
            dot(place[mi], c_slots[...].reshape(SLOTS, 512)),
            dot(place_out, c_slots2[...].reshape(SLOTS, 512)),
        )

        wait("w3")
        wait("m")
        to_sib("ms", my_rows, mixed_pair.at[1], ms_s, ms_r)
        rows_val = mixed_pair[0]
        for h in range(2):
            v = dot(rows_val, whole_w[h].reshape(D, 512))
            k0 = 0.7978845608028654
            th = jnp.tanh(k0 * (v + 0.044715 * (v * v * v)))
            act = 0.5 * v * (1.0 + th)
            slope = 0.5 * (1.0 + th) + 0.5 * v * (1.0 - th * th) * (k0 * (1.0 + 3 * 0.044715 * (v * v)))
            g_half[h] = (own_cot[h] * slope).astype(BF)
            out_ref[:, h * 512:(h + 1) * 512] = act.astype(BF)

        to_sib("g", g_half.at[1 - core], g_pair.at[1], g_s, g_r)
        g_pair[0] = g_half[core]

        for f in range(NI):
            w_rows = whole_w[:, f // 2, f % 2 * 2:f % 2 * 2 + 2]
            gf_out[f] = (
                dot_t1(g_half[0], w_rows[0].reshape(128, 512))
                + dot_t1(g_half[1], w_rows[1].reshape(128, 512))
            ).astype(BF)
        to_in("gf", lambda i: gf_out.at[i], gf_in.at[mi], gf_s, gf_r, gf_out.at[seven], gf_in.at[seven])
        gf_in[mi] = gf_out[mi]

        o_slots[...] = dot_t0(place_out, out_ref[:, :512]).astype(BF).reshape(NG, 16, 512)
        to_grp("o1", o_slots, o_mid, o1_s, o1_r)
        o_mid[mg] = o_slots[mg]
        p_slots[...] = dot_t0(place[mi], out_ref[:, 512:]).astype(BF).reshape(NI, 32, 512)
        to_in("p1", lambda i: p_slots.at[i], p_mid.at[mi], p1_s, p1_r, p_slots.at[seven], p_mid.at[seven])
        p_mid[mi] = p_slots[mi]

        wait("ms")
        wait("g")
        m_val = mixed_pair[...].reshape(2 * ROWS, D)
        for h in range(2):
            term = dot_t0(m_val, g_pair[:, :, h * 256:(h + 1) * 256].reshape(2 * ROWS, 256))
            term = term.astype(BF).reshape(4, 4, 64, 256)
            for n in range(4):
                if h == 0:
                    wa[n] = term[:, n]
                else:
                    wb[n] = term[n]
        to_four("ra", "x", lambda n: wa.at[n], wa_in.at[my_x], ra_s, ra_r, wa.at[three], wa.at[three])
        to_four("rb", "z", lambda n: wb.at[n], wb_in.at[my_z], rb_s, rb_r, wb.at[three], wb.at[three])
        wa_in[my_x] = wa[my_x]
        wb_in[my_z] = wb[my_z]

        wait("gf")
        feed = gf_in[...].reshape(D, 128)
        back = dot(adj[...], feed).astype(BF)
        for o in range(NI):
            z_slots[:, o] = (
                dot(place_t[o], back[o * 128:(o + 1) * 128]).astype(BF).reshape(NI, 32, 128)
            )
        for h in range(2):
            rows_h = pl.ds(pl.multiple_of(side(h) * 16, 16), 16)
            to_in(
                "z1%d" % h, lambda i: z_slots.at[i, :, rows_h], z_mid.at[mi, :, rows_h],
                z1_s.at[h], z1_r.at[h], z_slots.at[seven, :, rows_h], z_mid.at[seven, :, rows_h],
            )
        z_mid[mi] = z_slots[mi]


        def add(ref):
            out = ref[0].astype(F32)
            for n in range(1, 4):
                out = out + ref[n].astype(F32)
            return out

        wait("p1")
        p_send[...] = dot(perm_t, p_mid[...].reshape(SLOTS, 512)).astype(BF).reshape(NG, 16, 512)
        to_grp("p2", p_send, p_back, p2_s, p2_r)
        p_back[mg] = p_send[mg]

        wait("o1")
        o_send[...] = dot(perm, o_mid[...].reshape(SLOTS, 512)).astype(BF).reshape(NI, 32, 512)
        to_in("o2", lambda i: o_send.at[i], o_back.at[mi], o2_s, o2_r, o_send.at[seven], o_back.at[seven])
        o_back[mi] = o_send[mi]

        wait("ra")
        wa_sum[...] = add(wa_in).astype(BF)
        wait("rb")
        wb_sum[...] = add(wb_in).astype(BF)
        part = wa_sum.at[three]
        to_four("ra2", "z", lambda n: wa_sum.at[n], wa_in2.at[my_z], ra2_s, ra2_r, part, part)
        to_four("rb2", "x", lambda n: wb_sum.at[n], wb_in2.at[my_x], rb2_s, rb2_r, part, part)
        wa_in2[my_z] = wa_sum[my_z]
        wb_in2[my_x] = wb_sum[my_x]

        pz_r, pz_c = iota((ROWS, ROWS), 0), iota((ROWS, ROWS), 1)
        perm_z = ones_where(
            pz_c == jnp.bitwise_and(lax.shift_right_logical(pz_r, 1), 7) * 16
            + lax.shift_right_logical(pz_r, 4) * 2 + jnp.bitwise_and(pz_r, 1)
        )
        for h in range(2):
            wait("z1%d" % h)
            n_side = side(h)
            rows_h = pl.ds(pl.multiple_of(n_side * 16, 16), 16)
            for f in range(NI):
                z_send[pl.ds(n_side * 8, 8), :, f * 128:(f + 1) * 128] = (
                    dot(perm_z, z_mid[f, :, rows_h].reshape(ROWS, 128))
                    .astype(BF).reshape(8, 16, 128)
                )

            def go(p, carry):
                n = jnp.bitwise_and(my_gz + p, 7)
                dest = lax.div(n, 4) * 8 + n_side * 4 + lax.rem(n, 4)

                @pl.when(dest != mg)
                def _():
                    rcopy(z_send.at[n_side * 8 + n], z_back.at[mg], z2_s, z2_r, (dest, mi)).start()

                return carry

            lax.fori_loop(0, 8, go, 0)
        leaves(z_send.at[pl.ds(0, NG - 1)], z2_s)
        arrives("z2", z_back.at[pl.ds(0, NG - 1)], z2_r)
        z_back[mg] = z_send[lax.rem(my_z, 2) * 8 + my_gz]

        wait("ra2")
        wait("rb2")
        wy[:, :, :256] = add(wa_in2).reshape(NI, 8, 256)
        wy[:, :, 256:] = add(wb_in2).reshape(NI, 8, 256)
        to_in("ry", lambda i: wy.at[i], wy_in.at[mi], ry_s, ry_r, wy.at[seven], wy_in.at[seven])
        wy_in[mi] = wy[mi]
        wait("o2")
        out_ref[:, :512] = dot(collect_out, o_back[...].reshape(SLOTS, 512)).astype(BF)
        wait("p2")
        out_ref[:, 512:] = dot(collect, p_back[...].reshape(SLOTS, 512)).astype(BF)
        wait("ry")
        for c in range(2):
            half = wy_in[c]
            for n in range(1, 4):
                half = half + wy_in[2 * n + c]
            wgrad_ref[:, c * 512:(c + 1) * 512] = half * (1.0 / 128)
        wait("z2")
        grad_ref[...] = dot(collect, z_back[...].reshape(SLOTS, D)).astype(BF)

    body()
    for name in list(arriving):
        wait(name)
    for done in leaving:
        done()


def hand_over(a, b, c, a_out, b_out, c_out, sem):
    copies = [
        pltpu.make_async_copy(src, dst, sem.at[n])
        for n, (src, dst) in enumerate([(a, a_out), (b, b_out), (c, c_out)])
    ]
    for copy in copies:
        copy.start()
    for copy in copies:
        copy.wait()


def scratch():
    v = pltpu.VMEM
    dma = pltpu.SemaphoreType.DMA
    big, small = v((4, 4, 64, 256), BF), v((4, 64, 256), BF)
    grp_rows = v((NG, 16, D), BF)
    grp_half, in_half = v((NG, 16, 512), BF), v((NI, 32, 512), BF)
    bufs = [
        pltpu.SMEM((1, 10), I32),
        v((1, ROWS), I32), v((1, ROWS), I32), pltpu.SMEM((1,), I32), v((ROWS, D), BF), v((ROWS, D), BF), v((8, D), BF), v((1, 10, ROWS, ROWS), BF),
        grp_rows, grp_rows, v((NG, 16, ROWS), BF), v((NG, 16, ROWS), BF),
        grp_half, grp_half, in_half, in_half,
        v((8, D), F32), v((8, D), F32), v((2, 4, 4, 4, 16, 512), BF), v((NI, 5, ROWS, ROWS), BF),
        v((D, D), BF),
        v((NI, NI, 32, 128), BF), v((NI, NI, 32, 128), BF), v((NI, 16, SLOTS), BF),
        in_half, in_half, grp_half, grp_half, v((NI, ROWS, SLOTS), BF), v((NI, SLOTS, ROWS), BF),
        v((NI, ROWS, 128), BF), v((2, ROWS, D), BF),
        v((2, ROWS, 512), BF), v((2, ROWS, 512), BF), v((NI, ROWS, 128), BF), v((NI, ROWS, 128), BF),
        grp_half, grp_half, in_half, in_half, in_half, in_half, grp_half, grp_half,
        v((NI, NI, 32, 128), BF), v((NI, NI, 32, 128), BF), grp_rows, grp_rows,
        big, big, big, big, small, small, small, small, v((NI, 8, 512), F32), v((NI, 8, 512), F32),
    ]
    one, two, four, five = dma, dma((2,)), dma((4,)), dma((5,))
    sems = [dma((8,))]
    for s in [one] * 5 + [four] + [one] + [five, four] + [one] * 9 + [two] + [one] * 10:
        sems += [s, s]
    return bufs + sems


def per_device(
    encoded, owner_slot, label_mask, cotangent, weight, block_cols, block_counts, block_values
):
    anywhere = pl.BlockSpec(memory_space=pl.ANY)
    vm = pl.BlockSpec(memory_space=pltpu.VMEM)
    results = pl.pallas_call(
        kernel,
        out_shape=(
            pltpu.VMEM((ROWS, D), BF), pltpu.VMEM((ROWS, D), BF), pltpu.VMEM((8, D), F32),
        ),
        in_specs=[anywhere] * 8,
        out_specs=(vm,) * 3,
        scratch_shapes=scratch(),
        compiler_params=pltpu.CompilerParams(
            collective_id=0, has_side_effects=True, vmem_limit_bytes=58 * 1024 * 1024
        ),
    )(
        block_cols, owner_slot.reshape(1, ROWS), label_mask.reshape(1, ROWS),
        block_counts, encoded, cotangent, weight, block_values,
    )
    return tuple(pl.pallas_call(
        hand_over,
        out_shape=tuple(jax.ShapeDtypeStruct(r.shape, r.dtype) for r in results),
        in_specs=[vm] * 3,
        out_specs=(anywhere,) * 3,
        scratch_shapes=[pltpu.SemaphoreType.DMA((3,))],
    )(*[pltpu.with_memory_space_constraint(r, pltpu.VMEM) for r in results]))


def solution(mesh):
    rows = P(("grp", "in"), None)
    flat = P(("grp", "in"))
    in_specs = (rows, flat, flat, rows, rows, rows, flat, P(("grp", "in"), None, None, None))
    return jax.shard_map(
        per_device, mesh=mesh, in_specs=in_specs, out_specs=(rows, rows, rows), check_vma=False
    )
```

```python
import functools

import jax
import jax.numpy as jnp
from jax import lax
from jax.experimental import pallas as pl
from jax.experimental.pallas import tpu as pltpu
from jax.sharding import PartitionSpec as P

MESH = pl.DeviceIdType.MESH
BF = jnp.bfloat16
F32 = jnp.float32
I32 = jnp.int32

NG = 16
NI = 8
ROWS = 128
D = 1024
SLOTS = 256


def iota(shape, dim):
    return lax.broadcasted_iota(I32, shape, dim)


def ones_where(cond):
    return jnp.where(cond, 1.0, 0.0).astype(BF)


def dot(a, b):
    return jnp.dot(a, b, preferred_element_type=F32)


def dot_t0(a, b):
    return lax.dot_general(a, b, (((0,), (0,)), ((), ())), preferred_element_type=F32)


def dot_t1(a, b):
    return lax.dot_general(a, b, (((1,), (1,)), ((), ())), preferred_element_type=F32)


def kernel(
    cols_hbm, slot_hbm, mask_hbm, count_hbm, enc_hbm, cot_hbm, w_hbm, val_hbm,
    out_ref, grad_ref, wgrad_ref,
    cols_ref, slot_ref, mask_ref, count_ref, enc_ref, cot_ref, w_ref, val_ref,
    s_rows, r_rows, s_pl, r_pl, s_cot, r_cot, s_cot2, r_cot2,
    w_f32, w_got, whole_w, adj_up, adj,
    q_rows, x_slots, v_all, q_cot, c_slots, q_cot2, c_slots2, place, place_t,
    mixed, mixed_pair,
    g_half, g_pair, gf_out, gf_in,
    o_slots, o_mid, o_send, o_back,
    p_slots, p_mid, p_send, p_back,
    z_slots, z_mid, z_send, z_back,
    wa, wb, wa_in, wb_in, wa_sum, wb_sum, wa_in2, wb_in2, wy, wy_in,
    load,
    rows_s, rows_r, pl_s, pl_r, cot_s, cot_r,
    w0_s, w0_r, w1_s, w1_r, w2_s, w2_r, w3_s, w3_r,
    a_s, a_r, f_s, f_r,
    x_s, x_r, v_s, v_r, c_s, c_r,
    m_s, m_r, ms_s, ms_r,
    g_s, g_r, gf_s, gf_r,
    o1_s, o1_r, o2_s, o2_r,
    z1_s, z1_r, z2_s, z2_r,
    ra_s, ra_r, rb_s, rb_r, ra2_s, ra2_r, rb2_s, rb2_r, ry_s, ry_r,
    cot2_s, cot2_r, c2_s, c2_r, p1_s, p1_r, p2_s, p2_r,
):
    mg = lax.axis_index("grp")
    mi = lax.axis_index("in")
    core = lax.rem(mi, 2)
    my_y = lax.div(mi, 2)
    sib = mi + 1 - 2 * core

    arriving, leaving = {}, []

    def rcopy(src, dst, ss, rs, dev):
        return pltpu.make_async_remote_copy(
            src_ref=src, dst_ref=dst, send_sem=ss, recv_sem=rs, device_id=dev, device_id_type=MESH
        )

    def each(n, body):
        def step(p, carry):
            body(p)
            return carry

        lax.fori_loop(1, n, step, 0)

    def arrives(name, ref, rs):
        arriving[name] = lambda: rcopy(ref, ref, rs, rs, (mg, sib)).wait_recv()

    def leaves(ref, ss):
        leaving.append(lambda: rcopy(ref, ref, ss, ss, (mg, sib)).wait_send())

    def wait(name):
        arriving.pop(name)()

    def grp_to(p):
        return lax.rem(mg + 7 * p, NG)

    def in_to(p):
        return lax.rem(mi + 3 * p, NI)

    def y_to(q):
        return lax.rem(mi + 2 * q, NI)

    def y_from(q):
        return lax.rem(mi + NI - 2 * q, NI)

    def to_grp(name, src, dst, ss, rs):
        def go(p):
            rcopy(src.at[grp_to(p)], dst.at[mg], ss, rs, (grp_to(p), mi)).start()

        each(NG, go)
        leaves(src.at[pl.ds(0, NG - 1)], ss)
        arrives(name, dst.at[pl.ds(0, NG - 1)], rs)

    def to_in(name, src, dst, ss, rs, left, came):
        def go(p):
            rcopy(src(in_to(p)), dst, ss, rs, (mg, in_to(p))).start()

        each(NI, go)
        leaves(left, ss)
        arrives(name, came, rs)

    my_z, my_x = lax.div(mg, 4), lax.rem(mg, 4)
    my_gz = lax.div(my_z, 2) * 4 + my_x

    def to_four(name, axis, src, dst, ss, rs, left, came):
        for q in range(1, 4):
            if axis == "x":
                n = lax.rem(my_x + q, 4)
                dev = (my_z * 4 + n, mi)
            elif axis == "z":
                n = lax.rem(my_z + q, 4)
                dev = (n * 4 + my_x, mi)
            else:
                n = lax.rem(my_y + q, 4)
                dev = (mg, n * 2 + core)
            rcopy(src(n), dst, ss, rs, dev).start()
        leaves(left, ss)
        arrives(name, came, rs)

    def to_sib(name, src, dst, ss, rs, came=None):
        rcopy(src, dst, ss, rs, (mg, sib)).start()
        leaves(src, ss)
        arrives(name, dst if came is None else came, rs)

    loads = [
        pltpu.make_async_copy(src, dst, load.at[n])
        for n, (src, dst) in enumerate(
            [(enc_hbm, enc_ref), (w_hbm, w_ref), (val_hbm, val_ref), (cot_hbm, cot_ref), (count_hbm, count_ref),
             (cols_hbm, cols_ref), (slot_hbm, slot_ref), (mask_hbm, mask_ref)]
        )
    ]
    for n in (6, 0, 1, 2, 4, 5, 7, 3):
        loads[n].start()

    seven = pl.ds(0, NI - 1)

    def side(h):
        return lax.rem(my_z + h, 2)

    barrier = pltpu.get_barrier_semaphore()

    def greet(dev):
        pl.semaphore_signal(barrier, inc=1, device_id=dev, device_id_type=MESH)

    each(NG, lambda p: greet((grp_to(p), mi)))
    each(NI, lambda p: greet((mg, in_to(p))))

    def body():
        loads[6].wait()
        slot_row = slot_ref[...]
        eye = iota((ROWS, ROWS), 0) == iota((ROWS, ROWS), 1)
        slot_b = jnp.broadcast_to(slot_row, (ROWS, ROWS))
        slot_col = jnp.sum(jnp.where(eye, slot_b, 0), axis=1, keepdims=True)
        own_b = lax.shift_right_logical(slot_b, 7)
        own_col = lax.shift_right_logical(slot_col, 7)
        same = own_b == jnp.broadcast_to(own_col, (ROWS, ROWS))
        n_ix, m_ix = iota((ROWS, ROWS), 0), iota((ROWS, ROWS), 1)
        rank_row = jnp.sum(jnp.where(same & (n_ix < m_ix), 1, 0), axis=0, keepdims=True)
        rank_col = jnp.sum(jnp.where(same & (m_ix < n_ix), 1, 0), axis=1, keepdims=True)
        flat_row = lax.shift_right_logical(slot_row, 7) * 2 + rank_row
        flat_col = own_col * 2 + rank_col
        spread = iota((SLOTS, ROWS), 0) == jnp.broadcast_to(flat_row, (SLOTS, ROWS))
        spread_rows = ones_where(spread)
        place1 = jnp.bitwise_and(slot_col, ROWS - 1) + 1
        place_b = jnp.broadcast_to(place1, (ROWS, ROWS)).astype(F32).astype(BF)
        s_pl[...] = dot(spread_rows, place_b).astype(BF).reshape(NG, 16, ROWS)
        loads[0].wait()
        s_rows[...] = dot(spread_rows, enc_ref[...]).astype(BF).reshape(NG, 16, D)

        pl.semaphore_wait(barrier, (NG - 1) + (NI - 1))
        to_grp("pl", s_pl, r_pl, pl_s, pl_r)
        to_grp("rows", s_rows, r_rows, rows_s, rows_r)
        r_rows[mg] = s_rows[mg]

        r_pl[mg] = s_pl[mg]
        loads[1].wait()
        w_f32[...] = w_ref[...].astype(F32)
        to_sib("w0", w_f32, w_got, w0_s, w0_r)

        loads[2].wait()
        loads[4].wait()
        loads[5].wait()
        count = count_ref[0]
        for j in range(5):
            col = lax.rem(mi + j, NI)
            acc = jnp.zeros((ROWS, ROWS), F32)
            for k in range(10):
                live = jnp.logical_and(cols_ref[0, k] == col, count > k)
                acc = acc + val_ref[0, k].astype(F32) * jnp.where(live, 1.0, 0.0)
            adj_up[mi, j] = acc.astype(BF)
        wait("w0")
        first = core == 0
        pair = jnp.concatenate(
            [
                jnp.where(first, w_f32[...], w_got[...]),
                jnp.where(first, w_got[...], w_f32[...]),
            ],
            axis=0,
        )
        pair = jnp.where(first, pair[:, :512], pair[:, 512:]).astype(BF)
        mine_w = whole_w.at[core, my_z, my_x, my_y]
        mine_w[...] = pair
        to_four(
            "w1", "y", lambda n: mine_w, mine_w, w1_s, w1_r,
            whole_w.at[core, 0, 0, pl.ds(0, 3)], whole_w.at[core, 0, 0, pl.ds(0, 3)],
        )

        mine_up = adj_up.at[mi]
        for q in (1, 3):
            rcopy(mine_up, mine_up, a_s.at[q], a_r.at[q], (mg, y_to(q))).start()
            leaves(mine_up, a_s.at[q])
            arrives("a%d" % q, mine_up, a_r.at[q])
        to_sib("a0", mine_up, mine_up, a_s.at[0], a_r.at[0])


        loads[7].wait()
        labelled = mask_ref[...] > 0
        spread_cot = ones_where(spread & jnp.broadcast_to(labelled, (SLOTS, ROWS)))

        def even_first(g):
            return (
                jnp.bitwise_and(g, 4) * 2
                + lax.shift_right_logical(jnp.bitwise_and(g, 8), 1)
                + jnp.bitwise_and(g, 3)
            )

        own_row = lax.shift_right_logical(slot_row, 7)
        flat_in = (
            jnp.bitwise_and(own_row, 7) * 32
            + even_first(lax.shift_right_logical(own_row, 3)) * 2 + rank_row
        )
        spread_in = ones_where(
            iota((SLOTS, ROWS), 0)
            == jnp.broadcast_to(jnp.where(labelled, flat_in, -1), (SLOTS, ROWS))
        )
        loads[3].wait()
        s_cot2[...] = dot(spread_in, cot_ref[:, 512:]).astype(BF).reshape(NI, 32, 512)
        to_in(
            "cot2", lambda i: s_cot2.at[i], r_cot2.at[mi], cot2_s, cot2_r,
            s_cot2.at[seven], r_cot2.at[seven],
        )
        r_cot2[mi] = s_cot2[mi]
        s_cot[...] = dot(spread_cot, cot_ref[:, :512]).astype(BF).reshape(NG, 16, 512)
        to_grp("cot", s_cot, r_cot, cot_s, cot_r)
        r_cot[mg] = s_cot[mg]

        collect = ones_where(
            iota((ROWS, SLOTS), 1) == jnp.broadcast_to(flat_col, (ROWS, SLOTS))
        )
        flat_out = (
            jnp.bitwise_and(own_col, 7) * 32
            + even_first(lax.shift_right_logical(own_col, 3)) * 2 + rank_col
        )
        collect_out = ones_where(
            iota((ROWS, SLOTS), 1) == jnp.broadcast_to(flat_out, (ROWS, SLOTS))
        )

        r_ix, c_ix = iota((SLOTS, SLOTS), 0), iota((SLOTS, SLOTS), 1)

        def moved(ix):
            z = jnp.bitwise_and(lax.shift_right_logical(ix, 2), 2) + jnp.bitwise_and(
                lax.shift_right_logical(ix, 4), 1
            )
            x = jnp.bitwise_and(lax.shift_right_logical(ix, 1), 3)
            return (
                (z * 4 + x) * 16 + lax.shift_right_logical(ix, 5) * 2 + jnp.bitwise_and(ix, 1)
            )

        perm = ones_where(c_ix == moved(r_ix))
        perm_t = ones_where(r_ix == moved(c_ix))
        low = (jnp.bitwise_and(r_ix, 31) == jnp.bitwise_and(c_ix, 31)) & (
            lax.shift_right_logical(c_ix, 5) == mi
        )
        o_rows = ones_where(
            iota((16, SLOTS), 0) == lax.shift_right_logical(iota((16, SLOTS), 1), 5)
        )

        wait("pl")
        pl_cols = dot(perm, r_pl[...].reshape(SLOTS, ROWS))
        pl_wide = jnp.concatenate([pl_cols, pl_cols], axis=1)
        v_all[mi] = dot(o_rows, jnp.where(low, pl_wide, 0.0).astype(BF)).astype(BF)
        to_in("v", lambda i: v_all.at[mi], v_all.at[mi], v_s, v_r, v_all.at[seven], v_all.at[seven])

        three, left_w, right_w = pl.ds(0, 3), pl.ds(0, 256), pl.ds(256, 256)
        wait("w1")
        group_l = whole_w.at[core, my_z, my_x, :, :, left_w]
        group_r = whole_w.at[core, my_z, my_x, :, :, right_w]
        some = whole_w.at[core, 0, three, :, :, left_w]
        to_four("w2l", "x", lambda n: group_l, group_l, w2_s.at[0], w2_r.at[0], some, some)
        to_four("w2r", "z", lambda n: group_r, group_r, w2_s.at[1], w2_r.at[1], some, some)

        for q, h in ((1, 2), (3, 4)):
            wait("a%d" % q)
            ref = adj_up.at[y_from(q), :, pl.ds(0 if q == 1 else 64, 64)]
            rcopy(ref, ref, a_s.at[h], a_r.at[h], (mg, y_to(q))).start()
            leaves(ref, a_s.at[h])
            arrives("a%d" % h, ref, a_r.at[h])
        wait("rows")
        for f in range(NI):
            part = r_rows[:, :, f * 128:(f + 1) * 128].reshape(SLOTS, 128)
            q_rows[f] = dot(perm, part).astype(BF).reshape(NI, 32, 128)
        to_in(
            "x", lambda i: q_rows.at[i], x_slots.at[:, mi], x_s, x_r,
            q_rows.at[seven], x_slots.at[:, seven],
        )
        x_slots[:, mi] = q_rows[mi]

        wait("w2l")
        wait("w2r")
        plane_l = whole_w.at[core, my_z, :, :, :, left_w]
        plane_r = whole_w.at[core, :, my_x, :, :, right_w]
        some = whole_w.at[core, three, :, :, :, left_w]
        to_four("w3l", "z", lambda n: plane_l, plane_l, w2_s.at[2], w2_r.at[2], some, some)
        to_four("w3r", "x", lambda n: plane_r, plane_r, w2_s.at[3], w2_r.at[3], some, some)


        wait("cot2")
        q_cot2[...] = dot(perm_t, r_cot2[...].reshape(SLOTS, 512)).astype(BF).reshape(NG, 16, 512)
        to_grp("c2", q_cot2, c_slots2, c2_s, c2_r)
        c_slots2[mg] = q_cot2[mg]

        wait("a2")
        wait("a4")
        for q in range(1, 4):
            ref = adj_up.at[y_from(q)]
            to_sib(
                "f%d" % q, ref, ref, f_s.at[q], f_r.at[q],
                adj_up.at[lax.rem(sib + NI - 2 * q, NI)],
            )

        wait("v")
        v_sum = v_all[0].astype(F32)
        for i in range(1, NI):
            v_sum = v_sum + v_all[i].astype(F32)
        node1 = (iota((ROWS, SLOTS), 0) + 1).astype(F32)
        for o in range(NI):
            here = jnp.where(node1 == jnp.broadcast_to(v_sum[o:o + 1, :], (ROWS, SLOTS)), 1.0, 0.0)
            place[o] = here.astype(BF)
            place_t[o] = here.T.astype(BF)

        for name in ("a0", "f1", "f2", "f3"):
            wait(name)
        for r in range(NI):
            for j in range(5):
                c = (r + j) % NI
                adj[r * 128:(r + 1) * 128, c * 128:(c + 1) * 128] = adj_up[r, j]
                if 0 < j < 4:
                    flipped = adj_up[r, j].astype(F32).T.astype(BF)
                    adj[c * 128:(c + 1) * 128, r * 128:(r + 1) * 128] = flipped

        wait("cot")
        q_cot[...] = dot(perm, r_cot[...].reshape(SLOTS, 512)).astype(BF).reshape(NI, 32, 512)
        to_in(
            "c", lambda i: q_cot.at[i], c_slots.at[mi], c_s, c_r, q_cot.at[seven], c_slots.at[seven]
        )
        c_slots[mi] = q_cot[mi]

        wait("x")
        feats = jnp.concatenate(
            [dot(place[o], x_slots[o].reshape(SLOTS, 128)).astype(BF) for o in range(NI)], axis=0
        )
        mixed[...] = dot(adj[...], feats).astype(BF).reshape(NI, ROWS, 128)
        my_rows = mixed_pair.at[0]
        my_cols = pl.ds(pl.multiple_of(mi * 128, 128), 128)
        to_in(
            "m", lambda i: mixed.at[i], my_rows.at[:, my_cols], m_s, m_r,
            mixed.at[seven], my_rows.at[:, pl.ds(0, 7 * 128)],
        )
        my_rows[:, my_cols] = mixed[mi]

        wait("w3l")
        wait("w3r")
        to_sib("w3", whole_w.at[core], whole_w.at[core], w3_s, w3_r, whole_w.at[1 - core])

        wait("c")
        place_out = dot(place[mi], perm).astype(BF)
        wait("c2")
        own_cot = (
            dot(place[mi], c_slots[...].reshape(SLOTS, 512)),
            dot(place_out, c_slots2[...].reshape(SLOTS, 512)),
        )

        wait("w3")
        wait("m")
        to_sib("ms", my_rows, mixed_pair.at[1], ms_s, ms_r)
        rows_val = mixed_pair[0]
        for h in range(2):
            v = dot(rows_val, whole_w[h].reshape(D, 512))
            k0 = 0.7978845608028654
            th = jnp.tanh(k0 * (v + 0.044715 * (v * v * v)))
            act = 0.5 * v * (1.0 + th)
            slope = 0.5 * (1.0 + th) + 0.5 * v * (1.0 - th * th) * (k0 * (1.0 + 3 * 0.044715 * (v * v)))
            g_half[h] = (own_cot[h] * slope).astype(BF)
            out_ref[:, h * 512:(h + 1) * 512] = act.astype(BF)

        to_sib("g", g_half.at[1 - core], g_pair.at[1], g_s, g_r)
        g_pair[0] = g_half[core]

        for f in range(NI):
            w_rows = whole_w[:, f // 2, f % 2 * 2:f % 2 * 2 + 2]
            gf_out[f] = (
                dot_t1(g_half[0], w_rows[0].reshape(128, 512))
                + dot_t1(g_half[1], w_rows[1].reshape(128, 512))
            ).astype(BF)
        to_in("gf", lambda i: gf_out.at[i], gf_in.at[mi], gf_s, gf_r, gf_out.at[seven], gf_in.at[seven])
        gf_in[mi] = gf_out[mi]

        o_slots[...] = dot_t0(place_out, out_ref[:, :512]).astype(BF).reshape(NG, 16, 512)
        to_grp("o1", o_slots, o_mid, o1_s, o1_r)
        o_mid[mg] = o_slots[mg]
        p_slots[...] = dot_t0(place[mi], out_ref[:, 512:]).astype(BF).reshape(NI, 32, 512)
        to_in("p1", lambda i: p_slots.at[i], p_mid.at[mi], p1_s, p1_r, p_slots.at[seven], p_mid.at[seven])
        p_mid[mi] = p_slots[mi]

        wait("ms")
        wait("g")
        m_val = mixed_pair[...].reshape(2 * ROWS, D)
        for h in range(2):
            term = dot_t0(m_val, g_pair[:, :, h * 256:(h + 1) * 256].reshape(2 * ROWS, 256))
            term = term.astype(BF).reshape(4, 4, 64, 256)
            for n in range(4):
                if h == 0:
                    wa[n] = term[:, n]
                else:
                    wb[n] = term[n]
        to_four("ra", "x", lambda n: wa.at[n], wa_in.at[my_x], ra_s, ra_r, wa.at[three], wa.at[three])
        to_four("rb", "z", lambda n: wb.at[n], wb_in.at[my_z], rb_s, rb_r, wb.at[three], wb.at[three])
        wa_in[my_x] = wa[my_x]
        wb_in[my_z] = wb[my_z]

        wait("gf")
        feed = gf_in[...].reshape(D, 128)
        back = dot(adj[...], feed).astype(BF)
        for o in range(NI):
            z_slots[:, o] = (
                dot(place_t[o], back[o * 128:(o + 1) * 128]).astype(BF).reshape(NI, 32, 128)
            )
        for h in range(2):
            rows_h = pl.ds(pl.multiple_of(side(h) * 16, 16), 16)
            to_in(
                "z1%d" % h, lambda i: z_slots.at[i, :, rows_h], z_mid.at[mi, :, rows_h],
                z1_s.at[h], z1_r.at[h], z_slots.at[seven, :, rows_h], z_mid.at[seven, :, rows_h],
            )
        z_mid[mi] = z_slots[mi]


        def add(ref):
            out = ref[0].astype(F32)
            for n in range(1, 4):
                out = out + ref[n].astype(F32)
            return out

        wait("p1")
        p_send[...] = dot(perm_t, p_mid[...].reshape(SLOTS, 512)).astype(BF).reshape(NG, 16, 512)
        to_grp("p2", p_send, p_back, p2_s, p2_r)
        p_back[mg] = p_send[mg]

        wait("o1")
        o_send[...] = dot(perm, o_mid[...].reshape(SLOTS, 512)).astype(BF).reshape(NI, 32, 512)
        to_in("o2", lambda i: o_send.at[i], o_back.at[mi], o2_s, o2_r, o_send.at[seven], o_back.at[seven])
        o_back[mi] = o_send[mi]

        wait("ra")
        wa_sum[...] = add(wa_in).astype(BF)
        wait("rb")
        wb_sum[...] = add(wb_in).astype(BF)
        part = wa_sum.at[three]
        to_four("ra2", "z", lambda n: wa_sum.at[n], wa_in2.at[my_z], ra2_s, ra2_r, part, part)
        to_four("rb2", "x", lambda n: wb_sum.at[n], wb_in2.at[my_x], rb2_s, rb2_r, part, part)
        wa_in2[my_z] = wa_sum[my_z]
        wb_in2[my_x] = wb_sum[my_x]

        pz_r, pz_c = iota((ROWS, ROWS), 0), iota((ROWS, ROWS), 1)
        perm_z = ones_where(
            pz_c == jnp.bitwise_and(lax.shift_right_logical(pz_r, 1), 7) * 16
            + lax.shift_right_logical(pz_r, 4) * 2 + jnp.bitwise_and(pz_r, 1)
        )
        for h in range(2):
            wait("z1%d" % h)
            n_side = side(h)
            rows_h = pl.ds(pl.multiple_of(n_side * 16, 16), 16)
            for f in range(NI):
                z_send[pl.ds(n_side * 8, 8), :, f * 128:(f + 1) * 128] = (
                    dot(perm_z, z_mid[f, :, rows_h].reshape(ROWS, 128))
                    .astype(BF).reshape(8, 16, 128)
                )

            def go(p, carry):
                n = jnp.bitwise_and(my_gz + p, 7)
                dest = lax.div(n, 4) * 8 + n_side * 4 + lax.rem(n, 4)

                @pl.when(dest != mg)
                def _():
                    rcopy(z_send.at[n_side * 8 + n], z_back.at[mg], z2_s, z2_r, (dest, mi)).start()

                return carry

            lax.fori_loop(0, 8, go, 0)
        leaves(z_send.at[pl.ds(0, NG - 1)], z2_s)
        arrives("z2", z_back.at[pl.ds(0, NG - 1)], z2_r)
        z_back[mg] = z_send[lax.rem(my_z, 2) * 8 + my_gz]

        wait("ra2")
        wait("rb2")
        wy[:, :, :256] = add(wa_in2).reshape(NI, 8, 256)
        wy[:, :, 256:] = add(wb_in2).reshape(NI, 8, 256)
        to_in("ry", lambda i: wy.at[i], wy_in.at[mi], ry_s, ry_r, wy.at[seven], wy_in.at[seven])
        wy_in[mi] = wy[mi]
        wait("o2")
        out_ref[:, :512] = dot(collect_out, o_back[...].reshape(SLOTS, 512)).astype(BF)
        wait("p2")
        out_ref[:, 512:] = dot(collect, p_back[...].reshape(SLOTS, 512)).astype(BF)
        wait("ry")
        for c in range(2):
            half = wy_in[c]
            for n in range(1, 4):
                half = half + wy_in[2 * n + c]
            wgrad_ref[:, c * 512:(c + 1) * 512] = half * (1.0 / 128)
        while leaving:
            leaving.pop(0)()
        wait("z2")
        grad_ref[...] = dot(collect, z_back[...].reshape(SLOTS, D)).astype(BF)

    body()
    for name in list(arriving):
        wait(name)
    for done in leaving:
        done()


def hand_over(a, b, c, a_out, b_out, c_out, sem):
    copies = [
        pltpu.make_async_copy(src, dst, sem.at[n])
        for n, (src, dst) in enumerate([(a, a_out), (b, b_out), (c, c_out)])
    ]
    for copy in copies:
        copy.start()
    for copy in copies:
        copy.wait()


def scratch():
    v = pltpu.VMEM
    dma = pltpu.SemaphoreType.DMA
    big, small = v((4, 4, 64, 256), BF), v((4, 64, 256), BF)
    grp_rows = v((NG, 16, D), BF)
    grp_half, in_half = v((NG, 16, 512), BF), v((NI, 32, 512), BF)
    bufs = [
        pltpu.SMEM((1, 10), I32),
        v((1, ROWS), I32), v((1, ROWS), I32), pltpu.SMEM((1,), I32), v((ROWS, D), BF), v((ROWS, D), BF), v((8, D), BF), v((1, 10, ROWS, ROWS), BF),
        grp_rows, grp_rows, v((NG, 16, ROWS), BF), v((NG, 16, ROWS), BF),
        grp_half, grp_half, in_half, in_half,
        v((8, D), F32), v((8, D), F32), v((2, 4, 4, 4, 16, 512), BF), v((NI, 5, ROWS, ROWS), BF),
        v((D, D), BF),
        v((NI, NI, 32, 128), BF), v((NI, NI, 32, 128), BF), v((NI, 16, SLOTS), BF),
        in_half, in_half, grp_half, grp_half, v((NI, ROWS, SLOTS), BF), v((NI, SLOTS, ROWS), BF),
        v((NI, ROWS, 128), BF), v((2, ROWS, D), BF),
        v((2, ROWS, 512), BF), v((2, ROWS, 512), BF), v((NI, ROWS, 128), BF), v((NI, ROWS, 128), BF),
        grp_half, grp_half, in_half, in_half, in_half, in_half, grp_half, grp_half,
        v((NI, NI, 32, 128), BF), v((NI, NI, 32, 128), BF), grp_rows, grp_rows,
        big, big, big, big, small, small, small, small, v((NI, 8, 512), F32), v((NI, 8, 512), F32),
    ]
    one, two, four, five = dma, dma((2,)), dma((4,)), dma((5,))
    sems = [dma((8,))]
    for s in [one] * 5 + [four] + [one] + [five, four] + [one] * 9 + [two] + [one] * 10:
        sems += [s, s]
    return bufs + sems


def per_device(
    encoded, owner_slot, label_mask, cotangent, weight, block_cols, block_counts, block_values
):
    anywhere = pl.BlockSpec(memory_space=pl.ANY)
    vm = pl.BlockSpec(memory_space=pltpu.VMEM)
    results = pl.pallas_call(
        kernel,
        out_shape=(
            pltpu.VMEM((ROWS, D), BF), pltpu.VMEM((ROWS, D), BF), pltpu.VMEM((8, D), F32),
        ),
        in_specs=[anywhere] * 8,
        out_specs=(vm,) * 3,
        scratch_shapes=scratch(),
        compiler_params=pltpu.CompilerParams(
            collective_id=0, has_side_effects=True, vmem_limit_bytes=58 * 1024 * 1024
        ),
    )(
        block_cols, owner_slot.reshape(1, ROWS), label_mask.reshape(1, ROWS),
        block_counts, encoded, cotangent, weight, block_values,
    )
    return tuple(pl.pallas_call(
        hand_over,
        out_shape=tuple(jax.ShapeDtypeStruct(r.shape, r.dtype) for r in results),
        in_specs=[vm] * 3,
        out_specs=(anywhere,) * 3,
        scratch_shapes=[pltpu.SemaphoreType.DMA((3,))],
    )(*[pltpu.with_memory_space_constraint(r, pltpu.VMEM) for r in results]))


def solution(mesh):
    rows = P(("grp", "in"), None)
    flat = P(("grp", "in"))
    in_specs = (rows, flat, flat, rows, rows, rows, flat, P(("grp", "in"), None, None, None))
    return jax.shard_map(
        per_device, mesh=mesh, in_specs=in_specs, out_specs=(rows, rows, rows), check_vma=False
    )
```
